128 devices in a mesh: leaf: 128 (over z, y, x, core).
Axes of the slice: x: 4, y: 4, z: 4, core: 2. Of those that a mesh axis runs over, the one named last changes fastest.
Arguments:
- rhs: bfloat16 [8192, 64, 256], P('leaf'), may hold values from -6 to 6
- points: bfloat16 [8192, 3, 256], P('leaf'), may hold values from 0 to 0.099609375
- upward_leaf_bases: bfloat16 [8192, 64, 256], P('leaf'), may hold values from -0.375 to 0.375
- downward_leaf_bases: bfloat16 [8192, 64, 256], P('leaf'), may hold values from -0.5 to 0.5
- up_leaf: bfloat16 [8192, 64, 64], P('leaf'), may hold values from -0.25 to 0.25
- leaf_down_transfer: bfloat16 [8192, 64, 64], P('leaf'), may hold values from -0.5 to 0.5
- couple_leaf: bfloat16 [8192, 8, 64, 64], P('leaf'), may hold values from -0.25 to 0.25
- list_leaf: int32 [8192, 8], P('leaf'), may hold values from 0 to 8191, as said below
- count_leaf: int32 [8192], P('leaf'), may hold values from 1 to 8
- up_node: bfloat16 [1024, 64, 64], P('leaf'), may hold values from -0.25 to 0.25
- down_node: bfloat16 [1024, 64, 64], P('leaf'), may hold values from -0.5 to 0.5
- couple_node: bfloat16 [1024, 4, 64, 64], P('leaf'), may hold values from -0.375 to 0.375
- list_node: int32 [1024, 4], P('leaf'), may hold values from 0 to 1023, as said below
- count_node: int32 [1024], P('leaf'), may hold values from 1 to 4
- up_top: float32 [128, 5, 64, 64], P('leaf'), as said below
- down_top: float32 [128, 5, 64, 64], P('leaf'), as said below
- couple_top: float32 [128, 6, 4, 64, 64], P('leaf'), as said below
Outputs:
- applied: bfloat16 [8192, 64, 256], P('leaf')
The draws below stay inside these ranges and needn't reach their ends.
Inputs may be any that keep to these rules, and one draw needn't show every extreme that they name: For k < count_leaf[s], list_leaf[s, k] is a leaf 2 to 8 leaves away from s; for k >= count_leaf[s] it is s. For k < count_node[a], list_node[a, k] is a level-1 node 2 to 4 nodes away from a; for k >= count_node[a] it is a. up_top[d, h] is equal for all d with the same d // 2^h. down_top[d, h] is equal for all d with the same d // 2^h. couple_top[d, h] is equal for all d with the same d // 2^h.
All inputs are finite; a program needn't handle non-finite values.
Results may differ from the reference program's by a relative error of at most 0.0065.
Values may be sent and summed in bfloat16 or wider, within the bound.
No kernel may reach another device: no remote copies, remote signals or barrier semaphores. Data moves between devices by JAX's collectives and lax.ppermute only.
A program may use at most 192 MiB of HBM per device.

```python
import jax
import jax.numpy as jnp
from jax import lax

P_SIZE = 256
R = 64
S = 64
LEAVES_PER_BRANCH = 8
LD1 = 8
W0 = 8
K0 = 8
W1 = 4
K1 = 4
LEAVES_DEV = 64
LEAVES = 8192
NODES1 = 1024
DNODES = 128
TOPE = 5
TOPC = 6


def draw_lists(key, row_count, reach, slots):
    key_counts = jax.random.fold_in(key, 101)
    counts = jax.random.randint(key_counts, (row_count,), 1, slots + 1)
    first_row = jax.random.randint(jax.random.fold_in(key_counts, 1), (), 0, row_count)
    counts = counts.at[first_row].set(slots).at[(first_row + 1) % row_count].set(1)
    offset_table = jnp.concatenate([jnp.arange(-reach, -1), jnp.arange(2, reach + 1)]).astype(jnp.int32)
    width_table = offset_table.shape[0]
    scores = jax.random.randint(jax.random.fold_in(key, 202), (row_count, width_table), 0, 1 << 20) * 64 + jnp.arange(width_table)[None, :]
    ranked = jnp.argsort(scores, axis=1)[:, :slots]
    offsets = offset_table[ranked]
    own_row = jnp.arange(row_count, dtype=jnp.int32)[:, None]
    picked = own_row + offsets
    picked = jnp.where((picked < 0) | (picked >= row_count), own_row - offsets, picked)
    live_mask = jnp.arange(slots)[None, :] < counts[:, None]
    picked = jnp.where(live_mask, picked, own_row)
    return (picked.astype(jnp.int32), counts.astype(jnp.int32))


def replicate_levels(base_draw):
    height_count = base_draw.shape[0]
    node_total = base_draw.shape[1]
    owner_row = jnp.arange(node_total)[:, None] >> jnp.arange(height_count)[None, :]
    return base_draw[jnp.arange(height_count)[None, :], owner_row]


def draw_list_leaf(key, part):
    return draw_lists(jax.random.fold_in(key, 7), LEAVES, W0, K0)[0]


def draw_count_leaf(key, part):
    return draw_lists(jax.random.fold_in(key, 7), LEAVES, W0, K0)[1]


def draw_list_node(key, part):
    return draw_lists(jax.random.fold_in(key, 9), NODES1, W1, K1)[0]


def draw_count_node(key, part):
    return draw_lists(jax.random.fold_in(key, 9), NODES1, W1, K1)[1]


def draw_up_top(key, part):
    key = jax.random.fold_in(key, 31)
    base_draw = jax.random.normal(key, (TOPE, DNODES, R, R), jnp.float32) * (2.0 * R) ** (-0.5)
    return replicate_levels(base_draw)


def draw_down_top(key, part):
    key = jax.random.fold_in(key, 37)
    base_draw = jax.random.normal(key, (TOPE, DNODES, R, R), jnp.float32) * (2.0 * R) ** (-0.5)
    return replicate_levels(base_draw)


def draw_couple_top(key, part):
    key = jax.random.fold_in(key, 41)
    base_draw = jax.random.normal(key, (TOPC, DNODES, 4, R, R), jnp.float32) * (3.0 * R) ** (-0.5)
    return replicate_levels(base_draw)


def level_of(rng, extent, cuts, smallest, high):
    gain, own = 1.0, jax.random.fold_in(rng, 6)
    for axis_at, shards_of in cuts:
        draws = jnp.exp(jax.random.uniform(jax.random.fold_in(own, axis_at), (shards_of,), jnp.float32, smallest / len(cuts), high / len(cuts)))
        gain = gain * jnp.repeat(draws, extent[axis_at] // shards_of).reshape([-1 if axis == axis_at else 1 for axis in range(len(extent))])
    return gain


def bell_draw(own_key, shape, scale, most, split=(), kind=jnp.bfloat16):
    array = jax.random.normal(own_key, shape, jnp.float32) * scale
    if len(split) > 0:
        array = level_of(own_key, shape, split, -0.22, 0.18) * array
    return jnp.clip(array, min=-most, max=most).astype(kind)


def setup_inputs(seed: int = 0) -> dict:
    keys = jax.random.split(jax.random.key(seed), 18)
    rhs = bell_draw(keys[0], (LEAVES, S, P_SIZE), 1.0, 6.0, ((0, 128),))
    points = jnp.clip(0.099609375 * jax.random.uniform(keys[1], (LEAVES, 3, P_SIZE), jnp.float32) ** level_of(keys[1], (LEAVES, 3, P_SIZE), ((0, 128),), -0.2, 0.2), 0.0, 0.099609375).astype(jnp.bfloat16)
    upward_leaf_bases = bell_draw(keys[2], (LEAVES, R, P_SIZE), P_SIZE ** -0.5, 0.375, ((0, 128),))
    downward_leaf_bases = bell_draw(keys[3], (LEAVES, R, P_SIZE), (2 * R) ** -0.5, 0.5, ((0, 128),))
    up_leaf = bell_draw(keys[4], (LEAVES, R, R), (R * LEAVES_PER_BRANCH) ** -0.5, 0.25, ((0, 128),))
    leaf_down_transfer = bell_draw(keys[5], (LEAVES, R, R), (2 * R) ** -0.5, 0.5, ((0, 128),))
    couple_leaf = bell_draw(keys[6], (LEAVES, K0, R, R), (R * K0) ** -0.5, 0.25, ((0, 128),))
    list_leaf = draw_list_leaf(jax.random.fold_in(keys[17], 71), 0)
    count_leaf = draw_count_leaf(jax.random.fold_in(keys[17], 71), 0)
    up_node = bell_draw(keys[9], (NODES1, R, R), (R * LD1) ** -0.5, 0.25, ((0, 128),))
    down_node = bell_draw(keys[10], (NODES1, R, R), (2 * R) ** -0.5, 0.5, ((0, 128),))
    couple_node = bell_draw(keys[11], (NODES1, K1, R, R), (R * K1) ** -0.5, 0.375, ((0, 128),))
    list_node = draw_list_node(jax.random.fold_in(keys[17], 71), 0)
    count_node = draw_count_node(jax.random.fold_in(keys[17], 71), 0)
    up_top = draw_up_top(jax.random.fold_in(keys[17], 71), 0)
    down_top = draw_down_top(jax.random.fold_in(keys[17], 71), 0)
    couple_top = draw_couple_top(jax.random.fold_in(keys[17], 71), 0)
    return {"rhs": rhs, "points": points, "upward_leaf_bases": upward_leaf_bases, "downward_leaf_bases": downward_leaf_bases, "up_leaf": up_leaf, "leaf_down_transfer": leaf_down_transfer, "couple_leaf": couple_leaf, "list_leaf": list_leaf, "count_leaf": count_leaf, "up_node": up_node, "down_node": down_node, "couple_node": couple_node, "list_node": list_node, "count_node": count_node, "up_top": up_top, "down_top": down_top, "couple_top": couple_top}


core_square = 0.0004
highest_precision = lax.Precision.HIGHEST
partner_offsets = (-3, -2, 2, 3)

def rounded_output(values):
    return lax.optimization_barrier(values.astype(jnp.bfloat16)).astype(jnp.float32)

def kernel_block(source, target):
    summed = jnp.zeros((source.shape[0], source.shape[2], target.shape[2]), jnp.float32)
    for coordinate in range(3):
        spacing = source[:, coordinate, :, None] - target[:, coordinate, None, :]
        summed = summed + spacing * spacing
    return (1.0 / source.shape[2] * lax.rsqrt(summed + core_square)).astype(jnp.bfloat16)

def near_field(rhs, points):
    zero_rhs = jnp.zeros((1,) + rhs.shape[1:], rhs.dtype)
    padded_rhs = jnp.concatenate([zero_rhs, rhs, zero_rhs], axis=0)
    located = points.astype(jnp.float32)
    zero_points = jnp.zeros((1,) + located.shape[1:], jnp.float32)
    padded_points = jnp.concatenate([zero_points, located, zero_points], axis=0)

    def one_block(start):
        target = lax.dynamic_slice_in_dim(located, start, LEAVES_DEV, 0)
        summed = jnp.zeros((LEAVES_DEV, S, P_SIZE), jnp.float32)
        for offset in range(3):
            source = lax.dynamic_slice_in_dim(padded_points, start + offset, LEAVES_DEV, 0)
            values = lax.dynamic_slice_in_dim(padded_rhs, start + offset, LEAVES_DEV, 0)
            kernel = lax.optimization_barrier(kernel_block(source, target)).astype(jnp.float32)
            summed = summed + jnp.einsum('lsp,lpq->lsq', values.astype(jnp.float32), kernel)
        return summed
    starts = (jnp.arange(LEAVES // LEAVES_DEV) * LEAVES_DEV).astype(jnp.int32)
    return lax.map(one_block, starts).reshape(LEAVES, S, P_SIZE)

def couple_level(coeff, lists, counts, blocks):
    summed = jnp.zeros((lists.shape[0], S, R), jnp.float32)
    for slot_index in range(lists.shape[1]):
        picked = jnp.take(coeff, lists[:, slot_index], axis=0).astype(jnp.float32)
        live_mask = (slot_index < counts).astype(jnp.float32)[:, None, None]
        summed = summed + jnp.einsum('nsr,nrq->nsq', picked * live_mask, blocks[:, slot_index].astype(jnp.float32))
    return summed

def reference(rhs, points, upward_leaf_bases, downward_leaf_bases, up_leaf, leaf_down_transfer, couple_leaf, list_leaf, count_leaf, up_node, down_node, couple_node, list_node, count_node, up_top, down_top, couple_top):
    nearby_sum_total = near_field(rhs, points)
    leaf_coefficient = jnp.einsum('qjg,qfg->qjf', rhs.astype(jnp.float32), upward_leaf_bases.astype(jnp.float32)).astype(jnp.bfloat16)
    leaf_wide = lax.optimization_barrier(leaf_coefficient).astype(jnp.float32)
    grouped = leaf_wide.reshape(NODES1, LEAVES_PER_BRANCH, S, R)
    node_coeff = jnp.einsum('absr,abrq->asq', grouped, up_leaf.astype(jnp.float32).reshape(NODES1, LEAVES_PER_BRANCH, R, R)).astype(jnp.bfloat16)
    node_wide = lax.optimization_barrier(node_coeff).astype(jnp.float32)
    device_coeff = jnp.einsum('asr,arq->asq', node_wide, up_node.astype(jnp.float32)).reshape(DNODES, LD1, S, R).sum(axis=1)
    leaf_gain_factor = couple_level(leaf_coefficient, list_leaf, count_leaf, couple_leaf)
    node_gain = couple_level(node_coeff, list_node, count_node, couple_node)
    top_bits = int(DNODES).bit_length() - 1
    coeffs = [device_coeff]
    for height in range(1, top_bits - 1):
        stride = 2 ** (height - 1)
        matrices = up_top[::stride, height - 1]
        carry_up = jnp.einsum('nsr,nrq->nsq', coeffs[-1], matrices, precision=highest_precision)
        coeffs.append(carry_up.reshape(-1, 2, S, R).sum(axis=1))
    couple_sums = []
    for height in range(top_bits - 1):
        level_value = coeffs[height]
        node_count = level_value.shape[0]
        padded = jnp.pad(level_value, ((3, 3), (0, 0), (0, 0)))
        node_index = jnp.arange(node_count)
        matrices = couple_top[::2 ** height, height]
        summed = jnp.zeros_like(level_value)
        for slot_index, offset in enumerate(partner_offsets):
            partner = padded[3 + offset:3 + offset + node_count]
            valid = (node_index + offset >= 0) & (node_index + offset < node_count)
            if offset == -3:
                valid = valid & (node_index % 2 == 1)
            if offset == 3:
                valid = valid & (node_index % 2 == 0)
            product = jnp.einsum('nsr,nrq->nsq', partner, matrices[:, slot_index], precision=highest_precision)
            summed = summed + jnp.where(valid[:, None, None], product, 0.0)
        couple_sums.append(summed)
    down_value = couple_sums[top_bits - 2]
    for height in range(top_bits - 2, 0, -1):
        matrices = down_top[::2 ** (height - 1), height - 1]
        spread = jnp.repeat(down_value, 2, axis=0)
        down_value = couple_sums[height - 1] + jnp.einsum('nsr,nrq->nsq', spread, matrices, precision=highest_precision)
    spread = jnp.repeat(rounded_output(down_value), LD1, axis=0)
    node_output_value = rounded_output(node_gain + jnp.einsum('asr,arq->asq', spread, down_node.astype(jnp.float32)))
    leaf_output_value = rounded_output(leaf_gain_factor + jnp.einsum('han,hny->hay', jnp.repeat(node_output_value, LEAVES_PER_BRANCH, axis=0), leaf_down_transfer.astype(jnp.float32)))
    product_output = nearby_sum_total + jnp.einsum('gjo,gob->gjb', leaf_output_value, downward_leaf_bases.astype(jnp.float32))
    return product_output.astype(jnp.bfloat16)
```

```python
import functools

import jax
import jax.numpy as jnp
from jax import lax
from jax.experimental import pallas as pl
from jax.experimental.pallas import tpu as pltpu
from jax.sharding import PartitionSpec as P

bf16 = jnp.bfloat16
f32 = jnp.float32
core_square = 0.0004
W0 = 8
W1 = 4
LEAF_AT, NODE_AT, RHS_AT, COORD_AT, HALO_TILES = 0, 4, 6, 8, 9
CARRY_AT, COEFF_AT = 9, 10


def dot(a, b):
    return jnp.dot(a, b, preferred_element_type=f32)


def dot_rows(a, b):
    return lax.dot_general(a, b, (((1,), (1,)), ((), ())), preferred_element_type=f32)


def dot_columns(a, b):
    return lax.dot_general(a, b, (((0,), (0,)), ((), ())), preferred_element_type=f32)


def low_lanes(shape):
    return lax.broadcasted_iota(jnp.int32, shape, len(shape) - 1) < shape[-1] // 2


def join(low, high):
    return jnp.where(low_lanes(low.shape), low.astype(f32), high.astype(f32)).astype(bf16)


def twice(block):
    return jnp.concatenate([block, block], axis=1)


def split(wide):
    hi = wide.astype(bf16).astype(f32)
    return jnp.concatenate([hi, wide - hi], axis=1).astype(bf16)


def fused_halves(block):
    half = block.shape[1] // 2
    return block[:, :half] + block[:, half:]


def wide_dot(left, matrix_parts):
    weights = jnp.concatenate([matrix_parts, matrix_parts], axis=0)
    return fused_halves(dot(split(left), weights))


def call(body, out_shape, grid, in_specs, out_specs, scratch=(), name=None, aliases=None, mib=16):
    return pl.pallas_call(
        body,
        out_shape=out_shape,
        grid=grid,
        in_specs=in_specs,
        out_specs=out_specs,
        scratch_shapes=list(scratch),
        input_output_aliases=aliases or {},
        compiler_params=pltpu.CompilerParams(vmem_limit_bytes=mib * 2**20),
        name=name,
    )


def whole(array):
    rank = array.ndim
    return pl.BlockSpec(array.shape, lambda i, rank=rank: (0,) * rank)


def rows(array, count):
    rank = array.ndim
    return pl.BlockSpec((count,) + array.shape[1:], lambda i, rank=rank: (i,) + (0,) * (rank - 1))


def scalars():
    return pl.BlockSpec(memory_space=pltpu.SMEM)


def shape(dims, dtype):
    return jax.ShapeDtypeStruct(dims, dtype)


def coordinate_rows(points):
    count = points.shape[1]
    scaled = points.astype(f32) * 256.0
    square = jnp.sum(scaled * scaled, axis=0, keepdims=True)
    row = lax.broadcasted_iota(jnp.int32, (16, count), 0)
    padded = jnp.concatenate([scaled, jnp.zeros((13, count), f32)], axis=0)

    def fill(base, at, ones_at, value):
        hi = value.astype(bf16).astype(f32)
        mid = (value - hi).astype(bf16).astype(f32)
        low = value - hi - mid
        base = jnp.where(row == at, hi, base)
        base = jnp.where(row == at + 1, mid, base)
        base = jnp.where(row == at + 2, low, base)
        return jnp.where((row >= ones_at) & (row < ones_at + 3), 1.0, base)

    source = fill(-2.0 * padded, 6, 3, square + core_square * 65536.0)
    target = fill(padded, 3, 6, square)
    return source.astype(bf16), target.astype(bf16)


def upward_body(
    dev_ref, rhs_ref, points_ref, bases_ref, up_leaf_ref, up_node_ref, up_top_ref,
    leaf_ref, node_ref, source_ref, target_ref, inner_ref, outer_ref, total,
):
    step = pl.program_id(0)
    last = pl.num_programs(0) - 1
    odd = lax.rem(dev_ref[0], 2) == 1
    pairs = []
    for b in range(8):
        base = bases_ref[b]
        coeff = dot_rows(rhs_ref[b], jnp.concatenate([base, base], axis=0)).astype(bf16)
        leaf_ref[b] = coeff
        source, target = coordinate_rows(points_ref[:, b, :])
        source_ref[b] = source
        target_ref[b] = target
        if b % 2 == 1:
            pairs.append(join(before, coeff))
        before = coeff
    up = up_leaf_ref[...].reshape(512, 64)
    node = dot(jnp.concatenate(pairs, axis=1), up).astype(bf16)
    node_ref[step] = twice(node)
    part = dot(node, up_node_ref[0])

    @pl.when(step == 0)
    def _():
        total[...] = part

    @pl.when(step > 0)
    def _():
        total[...] += part

    def edge(message, leaf):
        for j in range(4):
            message[LEAF_AT + j] = pairs[j]
        message[RHS_AT] = rhs_ref[leaf, :, :128]
        message[RHS_AT + 1] = rhs_ref[leaf, :, 128:]
        message[COORD_AT, 0:16, :] = source_ref[leaf, :, :128]
        message[COORD_AT, 16:32, :] = source_ref[leaf, :, 128:]
        message[COORD_AT, 32:48, :] = target_ref[leaf, :, :128]
        message[COORD_AT, 48:64, :] = target_ref[leaf, :, 128:]

    def edge_nodes(message, first):
        for j in range(2):
            message[NODE_AT + j] = join(node_ref[first + 2 * j], node_ref[first + 2 * j + 1])

    @pl.when((step == 0) & odd)
    def _():
        edge(inner_ref, 0)

    @pl.when((step == 0) & ~odd)
    def _():
        edge(outer_ref, 0)

    @pl.when((step == last) & odd)
    def _():
        edge(outer_ref, 7)
        edge_nodes(outer_ref, 4)
        edge_nodes(inner_ref, 0)

    @pl.when((step == last) & ~odd)
    def _():
        edge(inner_ref, 7)
        edge_nodes(inner_ref, 4)
        edge_nodes(outer_ref, 0)

    @pl.when(step == last)
    def _():
        coeff = total[...]
        inner_ref[CARRY_AT] = split(wide_dot(coeff, split(up_top_ref[0, 0])))
        inner_ref[COEFF_AT] = twice(coeff).astype(bf16)


def upward(dev, rhs, points, bases, up_leaf, up_node, up_top):
    leaves = rhs.shape[0]
    groups = up_node.shape[0]
    outs = [
        shape((leaves, 64, 128), bf16),
        shape((groups, 64, 128), bf16),
        shape((leaves, 16, 256), bf16),
        shape((leaves, 16, 256), bf16),
        shape((HALO_TILES + 2, 64, 128), bf16),
        shape((HALO_TILES, 64, 128), bf16),
    ]
    return call(
        upward_body,
        outs,
        (groups,),
        [scalars(), rows(rhs, 8), pl.BlockSpec((3, 8, 256), lambda i: (0, i, 0)), rows(bases, 8), rows(up_leaf, 8), rows(up_node, 1), whole(up_top)],
        [rows(outs[0], 8), whole(outs[1]), rows(outs[2], 8), rows(outs[3], 8), whole(outs[4]), whole(outs[5])],
        [pltpu.VMEM((64, 64), f32)],
        name="upward",
        mib=60,
    )(dev, rhs, points, bases, up_leaf, up_node, up_top)


def merge(own_ref, got_ref, carry_at, coeff_at, bit, hold):
    sums = own_ref[carry_at].astype(f32) + got_ref[carry_at].astype(f32)
    parent = fused_halves(sums)
    hold[bit] = own_ref[coeff_at]
    hold[1 - bit] = got_ref[coeff_at]
    return parent, join(hold[0], hold[1])


def ordered(own, got, bit, hold):
    hold[bit] = own
    hold[1 - bit] = got
    return hold[0], hold[1]


def bit_of(dev_ref, height):
    return (dev_ref[0] >> height) & 1


def carried(parent, up_top_ref, height):
    return split(wide_dot(parent, split(up_top_ref[0, height])))


def level_0_body(dev_ref, own, got, up_top_ref, out, hold):
    parent, pair = merge(own, got, CARRY_AT, COEFF_AT, bit_of(dev_ref, 0), hold)
    out[0] = carried(parent, up_top_ref, 1)
    out[1] = twice(parent).astype(bf16)
    out[2] = pair


def level_1_body(dev_ref, own, got, up_top_ref, out, hold):
    bit = bit_of(dev_ref, 1)
    parent, pair = merge(own, got, 0, 1, bit, hold)
    out[0] = carried(parent, up_top_ref, 2)
    out[1] = twice(parent).astype(bf16)
    out[2] = pair
    out[3], out[4] = ordered(own[2], got[2], bit, hold)


def level_2_body(dev_ref, own, got, up_top_ref, out, up_out, down_out, hold):
    bit = bit_of(dev_ref, 2)
    parent, pair = merge(own, got, 0, 1, bit, hold)
    out[0] = carried(parent, up_top_ref, 3)
    out[1] = twice(parent).astype(bf16)
    down_out[0] = ordered(own[3], got[3], bit, hold)[0]
    up_out[0] = ordered(own[4], got[4], bit, hold)[1]
    down_out[1], up_out[1] = ordered(own[2], got[2], bit, hold)
    down_out[2] = pair
    up_out[2] = pair


def level_3_body(dev_ref, own, got, up_top_ref, out, hold):
    parent, pair = merge(own, got, 0, 1, bit_of(dev_ref, 3), hold)
    out[0] = carried(parent, up_top_ref, 4)
    out[1] = twice(parent).astype(bf16)
    out[2] = pair


def level_4_body(dev_ref, own, got, near_out, far_out, across_out, hold):
    bit = bit_of(dev_ref, 4)
    parent, pair = merge(own, got, 0, 1, bit, hold)
    first, second = ordered(own[2], got[2], bit, hold)
    odd = bit_of(dev_ref, 5)
    near_out[0], far_out[0] = ordered(second, first, odd, hold)
    near_out[1] = pair
    far_out[1] = pair
    coeff = twice(parent).astype(bf16)
    far_out[2] = coeff
    across_out[0] = coeff


def level_call(body, dev, own, got, up_top, tiles, name):
    outs = [shape((count, 64, 128), bf16) for count in tiles]
    ins = [own, got] + ([] if up_top is None else [up_top])
    return call(
        body,
        outs,
        (1,),
        [scalars()] + [whole(a) for a in ins],
        [whole(a) for a in outs],
        [pltpu.VMEM((2, 64, 128), bf16)],
        name=name,
    )(dev, *ins)


def prepare_body(dev_ref, couple_ref, down_ref, couple_out, down_out):
    for height in range(6):
        odd = bit_of(dev_ref, height)
        even = 1 - odd
        picks = ((even, None), (1, odd), (2, even), (2 + even, None))
        for at, (slot, live) in enumerate(picks):
            matrix = couple_ref[0, height, slot]
            if live is not None:
                matrix = jnp.where(jnp.full(matrix.shape, live, jnp.int32) > 0, matrix, 0.0)
            couple_out[height, 64 * at : 64 * at + 64, :] = split(matrix)
    for height in range(5):
        down_out[height] = split(down_ref[0, height])


def prepare(dev, couple_top, down_top):
    outs = [shape((6, 256, 128), bf16), shape((5, 64, 128), bf16)]
    return call(
        prepare_body,
        outs,
        (1,),
        [scalars(), whole(couple_top), whole(down_top)],
        [whole(a) for a in outs],
        name="prepare",
    )(dev, couple_top, down_top)


def sides(dev_ref):
    odd = bit_of(dev_ref, 0)
    return 1 - odd, odd


def near_body(
    first, last, count, devices, dev_ref, rhs_ref, rhs_before, rhs_after, source_ref, target_ref,
    source_before, target_after, *rest,
):
    if first or last:
        inner_ref, outer_ref = rest[:2]
        rest = rest[2:]
    out_ref, kernels, rim_rhs, rim_source, rim_target = rest[-5:]
    step = pl.program_id(0)
    steps = pl.num_programs(0)
    rim_rhs[0] = rhs_before[0]
    rim_rhs[1] = rhs_after[0]
    rim_source[...] = source_before[0]
    rim_target[...] = target_after[0]

    if first or last:
        inner_at, _ = sides(dev_ref)

        def from_halo(side):
            def read(halo):
                rim_rhs[side, :, :128] = halo[RHS_AT]
                rim_rhs[side, :, 128:] = halo[RHS_AT + 1]

                @pl.when(dev_ref[0] != (0 if side == 0 else devices - 1))
                def _():
                    if side == 0:
                        rim_source[:, :128] = halo[COORD_AT, 0:16, :]
                        rim_source[:, 128:] = halo[COORD_AT, 16:32, :]
                    else:
                        rim_target[:, :128] = halo[COORD_AT, 32:48, :]
                        rim_target[:, 128:] = halo[COORD_AT, 48:64, :]

            at = step == (0 if side == 0 else steps - 1)

            @pl.when(at & (inner_at == side))
            def _():
                read(inner_ref)

            @pl.when(at & (inner_at != side))
            def _():
                read(outer_ref)

        if first:
            from_halo(0)
        if last:
            from_halo(1)

    def kernel_of(source, target):
        return lax.rsqrt(dot_columns(source, target)).astype(bf16)

    def build(s):
        after = target_ref[s + 1] if s + 1 < count else rim_target[...]
        kernels[s % 2] = kernel_of(source_ref[s], jnp.concatenate([target_ref[s], after], axis=1))

    before = kernel_of(rim_source[...], target_ref[0])
    build(0)
    out_ref[0] = dot(rim_rhs[0], before)
    for s in range(count):
        if s + 1 < count:
            build(s + 1)
        kernel = kernels[s % 2]
        after = rhs_ref[s + 1] if s + 1 < count else rim_rhs[1]
        out_ref[s] += dot(rhs_ref[s], kernel[:, :256]) + dot_rows(after, kernel[:, 256:])
        if s + 1 < count:
            out_ref[s + 1] = dot(rhs_ref[s], kernel[:, 256:])


def near(dev, rhs, source, target, begin, steps, halos, total, name, count=8):
    leaves = rhs.shape[0]
    first = begin == 0
    last = (begin + steps) * count == leaves
    at = lambda array: pl.BlockSpec((count,) + array.shape[1:], lambda i: (begin + i, 0, 0))
    before = lambda array: pl.BlockSpec(
        (1,) + array.shape[1:], lambda i: (jnp.maximum((begin + i) * count - 1, 0), 0, 0)
    )
    after = lambda array: pl.BlockSpec(
        (1,) + array.shape[1:], lambda i: (jnp.minimum((begin + i + 1) * count, leaves - 1), 0, 0)
    )
    args = [dev, rhs, rhs, rhs, source, target, source, target]
    specs = [scalars(), at(rhs), before(rhs), after(rhs), at(source), at(target), before(source), after(target)]
    if first or last:
        args += halos
        specs += [whole(a) for a in halos]
    aliases = {}
    if total is not None:
        aliases = {len(args): 0}
        args.append(total)
        specs.append(pl.BlockSpec(memory_space=pl.ANY))
    out = shape(rhs.shape, f32)
    return call(
        functools.partial(near_body, first, last, count, lax.axis_size("leaf")),
        out,
        (steps,),
        specs,
        at(out),
        [
            pltpu.VMEM((2, 256, 512), bf16),
            pltpu.VMEM((2, 64, 256), bf16),
            pltpu.VMEM((16, 256), bf16),
            pltpu.VMEM((16, 256), bf16),
        ],
        name=name,
        aliases=aliases,
    )(*args)


def couple_body(
    dev_ref, list_ref, count_ref, node_list_ref, node_count_ref, leaf_ref, node_ref, inner_ref,
    outer_ref, blocks_ref, node_blocks_ref, gain_ref, node_gain_ref, leaf_hold, node_hold,
):
    step = pl.program_id(0)
    leaves = leaf_ref.shape[0]
    groups = node_ref.shape[0]

    @pl.when(step == 0)
    def _():
        leaf_hold[W0 : W0 + leaves] = leaf_ref[...]
        node_hold[W1 : W1 + groups] = node_ref[...]
        leaf_hold[leaves + 2 * W0] = jnp.zeros((64, 128), bf16)
        node_hold[groups + 2 * W1] = jnp.zeros((64, 128), bf16)
        inner_side, outer_side = sides(dev_ref)
        for halo, side in ((inner_ref, inner_side), (outer_ref, outer_side)):

            def unpack(hold, at, tile):
                pair = halo[tile].astype(f32)
                turned = pltpu.roll(pair, 64, 1)
                low = low_lanes(pair.shape)
                hold[at] = jnp.where(low, pair, turned).astype(bf16)
                hold[at + 1] = jnp.where(low, turned, pair).astype(bf16)

            for j in range(4):
                unpack(leaf_hold, side * (leaves + W0) + 2 * j, LEAF_AT + j)
            for j in range(2):
                unpack(node_hold, side * (groups + W1) + 2 * j, NODE_AT + j)

    def picked(hold, lists, counts, row, first, slots, nothing):
        tiles = []
        for j in range(slots // 2):
            pair = []
            for k in (2 * j, 2 * j + 1):
                live = k < counts[row]
                pair.append(hold[jnp.where(live, lists[k, row] - first, nothing)])
            tiles.append(join(*pair))
        return jnp.concatenate(tiles, axis=1)

    for b in range(8):
        row = step * 8 + b
        values = picked(
            leaf_hold, list_ref, count_ref, row, dev_ref[0] * leaves - W0, 8, leaves + 2 * W0
        )
        gain_ref[b] = dot(values, blocks_ref[b].reshape(512, 64))
    values = picked(
        node_hold, node_list_ref, node_count_ref, step, dev_ref[0] * groups - W1, 4, groups + 2 * W1
    )
    node_gain_ref[0] = dot(values, node_blocks_ref[0].reshape(256, 64))


def couple(dev, lists, counts, node_lists, node_counts, leaf, node, inner, outer, blocks, node_blocks):
    leaves, groups = leaf.shape[0], node.shape[0]
    outs = [shape((leaves, 64, 64), f32), shape((groups, 64, 64), f32)]
    return call(
        couple_body,
        outs,
        (groups,),
        [scalars()] * 5
        + [whole(leaf), whole(node), whole(inner), whole(outer), rows(blocks, 8), rows(node_blocks, 1)],
        [rows(outs[0], 8), rows(outs[1], 1)],
        [
            pltpu.VMEM((leaves + 2 * W0 + 1, 64, 128), bf16),
            pltpu.VMEM((groups + 2 * W1 + 1, 64, 128), bf16),
        ],
        name="couple",
    )(dev, lists, counts, node_lists, node_counts, leaf, node, inner, outer, blocks, node_blocks)


def downward_body(
    dev_ref, pair_ref, four_ref, before_ref, after_ref, sixteen_ref, near_ref, far_ref, across_ref,
    couple_ref, down_ref, down_node_ref, node_gain_ref, gain_ref, transfer_ref, bases_ref,
    sum_ref, out_ref, bank, node_value,
):
    step = pl.program_id(0)

    @pl.when(step == 0)
    def _():
        bank[0] = jnp.zeros((64, 128), bf16)
        bank[1] = pair_ref[2]
        for j in range(3):
            bank[2 + j] = four_ref[2 + j]
            bank[5 + j] = before_ref[j]
            bank[8 + j] = after_ref[j]
        bank[11] = sixteen_ref[2]
        bank[12] = near_ref[0]
        bank[13] = near_ref[1]
        bank[14] = far_ref[0]
        bank[15] = far_ref[1]
        d = dev_ref[0]
        q = d >> 5
        odd = q & 1
        bank[16 + odd] = across_ref[0]
        bank[17 - odd] = far_ref[2]
        bank[16] = join(bank[16], bank[17])
        pick = jnp.where
        even = lambda value: (value & 1) == 0
        m = d >> 1
        left = [pick(even(m), pick((m & 3) == 2, 4, 5), 1)]
        right = [pick(even(m), 1, pick((m & 3) == 1, 3, 8))]
        m = d >> 2
        left.append(pick(even(m), 6, 2))
        right.append(pick(even(m), 2, 9))
        left.append(7)
        right.append(10)
        m = d >> 4
        left.append(pick(even(m), pick(odd == 1, 12, pick(q == 2, 14, 0)), 11))
        right.append(pick(even(m), 11, pick(odd == 0, 12, pick(q == 1, 14, 0))))
        left.append(pick(odd == 1, 13, pick(q == 2, 15, 0)))
        right.append(pick(odd == 0, 13, pick(q == 1, 15, 0)))
        left.append(pick(q >= 2, 16, 0))
        right.append(pick(q >= 2, 0, 16))
        gains = [
            fused_halves(
                dot(jnp.concatenate([bank[left[h]], bank[right[h]]], axis=1), couple_ref[h])
            )
            for h in range(6)
        ]
        value = gains[5]
        for h in range(4, -1, -1):
            value = gains[h] + wide_dot(value, down_ref[h])
        rounded = value.astype(bf16)
        for a in range(8):
            node_value[a] = (node_gain_ref[a] + dot(rounded, down_node_ref[a])).astype(bf16)

    value = node_value[step]
    for b in range(8):
        leaf_value = (gain_ref[b] + dot(value, transfer_ref[b])).astype(bf16)
        out_ref[b] = (sum_ref[b] + dot(leaf_value, bases_ref[b])).astype(bf16)


def downward(dev, received, couple_parts, down_parts, down_node, node_gain, gain, transfer, bases, near_sum):
    fixed = list(received) + [couple_parts, down_parts, down_node, node_gain]
    moving = [gain, transfer, bases, near_sum]
    out = shape(bases.shape, bf16)
    return call(
        downward_body,
        out,
        (down_node.shape[0],),
        [scalars()] + [whole(a) for a in fixed] + [rows(a, 8) for a in moving],
        rows(out, 8),
        [pltpu.VMEM((18, 64, 128), bf16), pltpu.VMEM((8, 64, 64), bf16)],
        name="downward",
    )(dev, *fixed, *moving)


def tied(*values):
    return lax.optimization_barrier(values)


def shards(
    rhs, points, upward_leaf_bases, downward_leaf_bases, up_leaf, leaf_down_transfer, couple_leaf,
    list_leaf, count_leaf, up_node, down_node, couple_node, list_node, count_node, up_top, down_top,
    couple_top,
):
    device = lax.axis_index("leaf")
    devices = lax.axis_size("leaf")
    dev = device.astype(jnp.int32).reshape(1)

    def exchange(block, mask):
        return lax.ppermute(block, "leaf", [(i, i ^ mask) for i in range(devices)])

    def shifted(block, distance):
        route = [(i, i + distance) for i in range(devices) if 0 <= i + distance < devices]
        return lax.ppermute(block, "leaf", route)

    leaf, node, source, target, inner_out, outer_out = upward(
        dev, rhs, jnp.transpose(points, (1, 0, 2)), upward_leaf_bases, up_leaf, up_node, up_top
    )
    inner = exchange(inner_out, 1)
    outer = lax.ppermute(
        outer_out, "leaf",
        [(i, i + 1) for i in range(1, devices - 1, 2)] + [(i + 1, i) for i in range(1, devices - 1, 2)],
    )
    near_sum = near(dev, rhs, source, target, 2, 2, [], None, "near_a")
    inner, near_sum = tied(inner, near_sum)
    (level_1,) = level_call(level_0_body, dev, inner_out, inner, up_top, [3], "level_0")
    pair = exchange(level_1, 2)
    near_sum, _ = tied(near_sum, level_1)
    near_sum = near(dev, rhs, source, target, 4, 2, [], near_sum, "near_b")
    pair, near_sum = tied(pair, near_sum)
    (level_2,) = level_call(level_1_body, dev, level_1, pair, up_top, [5], "level_1")
    four = exchange(level_2, 4)
    near_sum, _ = tied(near_sum, level_2)
    near_sum = near(dev, rhs, source, target, 0, 2, [inner, outer], near_sum, "near_c")
    four, near_sum = tied(four, near_sum)
    level_3, up_out, down_out = level_call(
        level_2_body, dev, level_2, four, up_top, [2, 3, 3], "level_2"
    )
    eight = exchange(level_3, 8)
    before = shifted(up_out, 8)
    after = shifted(down_out, -8)
    near_sum, _ = tied(near_sum, level_3)
    near_sum = near(dev, rhs, source, target, 6, 2, [inner, outer], near_sum, "near_d")
    eight, near_sum = tied(eight, near_sum)
    (level_4,) = level_call(level_3_body, dev, level_3, eight, up_top, [3], "level_3")
    sixteen = exchange(level_4, 16)
    leaf, _ = tied(leaf, level_4)
    gain, node_gain = couple(
        dev, list_leaf.T, count_leaf, list_node.T, count_node, leaf, node, inner, outer,
        couple_leaf, couple_node,
    )
    sixteen, gain = tied(sixteen, gain)
    near_out, far_out, across_out = level_call(
        level_4_body, dev, level_4, sixteen, None, [2, 3, 1], "level_4"
    )
    beside = exchange(near_out, 32)
    across = exchange(across_out, 64)
    far = exchange(far_out, 96)
    couple_top, _ = tied(couple_top, near_out)
    couple_parts, down_parts = prepare(dev, couple_top, down_top)
    beside, across, far, couple_parts = tied(beside, across, far, couple_parts)
    return downward(
        dev, (pair, four, before, after, sixteen, beside, far, across), couple_parts, down_parts,
        down_node, node_gain, gain, leaf_down_transfer, downward_leaf_bases, near_sum,
    )


def solution(mesh):
    placed = tuple(P("leaf") for _ in range(17))
    return jax.shard_map(
        shards, mesh=mesh, in_specs=placed, out_specs=P("leaf"), check_vma=False
    )
```

```python
import functools

import jax
import jax.numpy as jnp
from jax import lax
from jax.experimental import pallas as pl
from jax.experimental.pallas import tpu as pltpu
from jax.sharding import PartitionSpec as P

bf16 = jnp.bfloat16
f32 = jnp.float32
core_square = 0.0004
W0 = 8
W1 = 4
LEAF_AT, NODE_AT, RHS_AT, COORD_AT, HALO_TILES = 0, 4, 6, 8, 9
CARRY_AT, COEFF_AT = 9, 10
CHUNKS = 4
PARTNERS = (2, 6, 8, 24, 32, 96)


def dot(a, b):
    return jnp.dot(a, b, preferred_element_type=f32)


def dot_rows(a, b):
    return lax.dot_general(a, b, (((1,), (1,)), ((), ())), preferred_element_type=f32)


def dot_columns(a, b):
    return lax.dot_general(a, b, (((0,), (0,)), ((), ())), preferred_element_type=f32)


def low_lanes(shape):
    return lax.broadcasted_iota(jnp.int32, shape, len(shape) - 1) < shape[-1] // 2


def join(low, high):
    return jnp.where(low_lanes(low.shape), low.astype(f32), high.astype(f32)).astype(bf16)


def twice(block):
    return jnp.concatenate([block, block], axis=1)


def split(wide):
    hi = wide.astype(bf16).astype(f32)
    return jnp.concatenate([hi, wide - hi], axis=1).astype(bf16)


def fused_halves(block):
    half = block.shape[1] // 2
    return block[:, :half] + block[:, half:]


def wide_dot(left, matrix_parts):
    weights = jnp.concatenate([matrix_parts, matrix_parts], axis=0)
    return fused_halves(dot(split(left), weights))


def call(body, out_shape, in_specs, out_specs, scratch=(), name=None, aliases=None, mib=24):
    return pl.pallas_call(
        body,
        out_shape=out_shape,
        in_specs=in_specs,
        out_specs=out_specs,
        scratch_shapes=list(scratch),
        input_output_aliases=aliases or {},
        compiler_params=pltpu.CompilerParams(vmem_limit_bytes=mib * 2**20),
        name=name,
    )


def held(*arrays):
    return [pl.BlockSpec(memory_space=pltpu.VMEM) for _ in arrays]


def stored(*arrays):
    return [pl.BlockSpec(memory_space=pltpu.HBM) for _ in arrays]


def scalars(count=1):
    return [pl.BlockSpec(memory_space=pltpu.SMEM)] * count


def shape(dims, dtype):
    return jax.ShapeDtypeStruct(dims, dtype)


def three_parts(value):
    hi = value.astype(bf16).astype(f32)
    mid = (value - hi).astype(bf16).astype(f32)
    return hi, mid, value - hi - mid


class Coordinates:
    def __init__(self, points, group):
        self.scaled = [points[j, group * 8 : group * 8 + 8, :].astype(f32) * 256.0 for j in range(3)]
        square = sum(x * x for x in self.scaled)
        self.parts = three_parts(square)
        self.plus_core = three_parts(square + core_square * 65536.0)

    def rows(self, b):
        row = lax.broadcasted_iota(jnp.int32, (16, self.scaled[0].shape[1]), 0)

        def stacked(values, ones_at):
            rows = jnp.where((row >= ones_at) & (row < ones_at + 3), 1.0, 0.0)
            for at, value in values:
                rows = jnp.where(row == at, value[b : b + 1], rows)
            return rows.astype(bf16)

        source = stacked(
            [(j, -2.0 * self.scaled[j]) for j in range(3)] + [(6 + j, self.plus_core[j]) for j in range(3)], 3
        )
        target = stacked(
            [(j, self.scaled[j]) for j in range(3)] + [(3 + j, self.parts[j]) for j in range(3)], 6
        )
        return source, target


def upward_body(
    dev_ref, rhs_ref, points_ref, bases_ref, up_leaf_ref, up_node_ref, up_top_ref,
    leaf_ref, node_ref, inner_ref, outer_ref,
    rhs, bases, up_leaf, points, up_node, up_top, sems, more_sems,
):
    groups = up_node_ref.shape[0]
    odd = lax.rem(dev_ref[0], 2) == 1

    leaves = rhs_ref.shape[0]
    chunk = leaves // CHUNKS

    def moves(c):
        at = pl.ds(c * chunk, chunk)
        return [
            pltpu.make_async_copy(rhs_ref.at[at], rhs.at[at], sems.at[0, c]),
            pltpu.make_async_copy(bases_ref.at[at], bases.at[at], sems.at[1, c]),
        ]

    others = [
        pltpu.make_async_copy(points_ref, points, more_sems.at[0]),
        pltpu.make_async_copy(up_node_ref, up_node, more_sems.at[1]),
        pltpu.make_async_copy(up_top_ref.at[0, 0], up_top, more_sems.at[2]),
        pltpu.make_async_copy(up_leaf_ref, up_leaf, more_sems.at[3]),
    ]
    others[0].start()
    for c in range(CHUNKS):
        for move in moves(c):
            move.start()
        if c == 0:
            others[3].start()
    others[1].start()
    others[2].start()
    for c in range(CHUNKS):
        for move in moves(c):
            move.wait()
        for leaf in range(c * chunk, (c + 1) * chunk):
            base = bases[leaf]
            leaf_ref[leaf] = dot_rows(rhs[leaf], jnp.concatenate([base, base], axis=0)).astype(bf16)

    others[3].wait()
    others[1].wait()
    nodes = []
    for g in range(groups):
        pairs = [join(leaf_ref[g * 8 + 2 * j], leaf_ref[g * 8 + 2 * j + 1]) for j in range(4)]
        up = up_leaf[g * 8 : g * 8 + 8].reshape(512, 64)
        nodes.append(twice(dot(jnp.concatenate(pairs, axis=1), up)).astype(bf16))
        node_ref[g] = nodes[g]
    pairs = [join(nodes[2 * j], nodes[2 * j + 1]) for j in range(groups // 2)]
    coeff = dot(jnp.concatenate(pairs, axis=1), up_node[...].reshape(groups * 64, 64))
    others[0].wait()
    others[2].wait()
    inner_ref[CARRY_AT] = split(wide_dot(coeff, split(up_top[...])))
    inner_ref[COEFF_AT] = twice(coeff).astype(bf16)

    def edge(message, first_leaf, leaf, first_node):
        for j in range(4):
            message[LEAF_AT + j] = join(leaf_ref[first_leaf + 2 * j], leaf_ref[first_leaf + 2 * j + 1])
        for j in range(2):
            message[NODE_AT + j] = join(node_ref[first_node + 2 * j], node_ref[first_node + 2 * j + 1])
        message[RHS_AT] = rhs[leaf, :, :128]
        message[RHS_AT + 1] = rhs[leaf, :, 128:]
        source, target = Coordinates(points, leaf // 8).rows(leaf % 8)
        message[COORD_AT, 0:16, :] = source[:, :128]
        message[COORD_AT, 16:32, :] = source[:, 128:]
        message[COORD_AT, 32:48, :] = target[:, :128]
        message[COORD_AT, 48:64, :] = target[:, 128:]

    @pl.when(odd)
    def _():
        edge(inner_ref, 0, 0, 0)
        edge(outer_ref, leaves - W0, leaves - 1, groups - W1)

    @pl.when(~odd)
    def _():
        edge(outer_ref, 0, 0, 0)
        edge(inner_ref, leaves - W0, leaves - 1, groups - W1)


def upward(dev, rhs, points, bases, up_leaf, up_node, up_top):
    leaves = rhs.shape[0]
    groups = up_node.shape[0]
    outs = [
        shape((leaves, 64, 128), bf16),
        shape((groups, 64, 128), bf16),
        shape((HALO_TILES + 2, 64, 128), bf16),
        shape((HALO_TILES, 64, 128), bf16),
    ]
    ins = [rhs, points, bases, up_leaf, up_node, up_top]
    return call(
        upward_body,
        outs,
        scalars() + stored(*ins),
        held(*outs),
        [
            pltpu.VMEM(rhs.shape, bf16),
            pltpu.VMEM(bases.shape, bf16),
            pltpu.VMEM(up_leaf.shape, bf16),
            pltpu.VMEM(points.shape, bf16),
            pltpu.VMEM(up_node.shape, bf16),
            pltpu.VMEM((64, 64), f32),
            pltpu.SemaphoreType.DMA((2, CHUNKS)),
            pltpu.SemaphoreType.DMA((4,)),
        ],
        name="upward",
        mib=56,
    )(dev, *ins)


def lowest(round_at):
    return 0 if round_at < 3 else 3


def fixed_tiles(round_at):
    return 2 if round_at < 5 else 6 - round_at


def first_at(height, round_at):
    if round_at == 6:
        return height - lowest(round_at)
    return fixed_tiles(round_at) + 2 * (height - lowest(round_at))


def last_at(height, round_at):
    if round_at == 6:
        return height - lowest(round_at)
    return fixed_tiles(round_at) + min(1 + 2 * (height - lowest(round_at)), 2 * (round_at - 1 - lowest(round_at)))


def tiles_of(round_at):
    heights = round_at - lowest(round_at)
    if round_at == 3:
        return fixed_tiles(round_at) + 3
    return fixed_tiles(round_at) + (heights if round_at == 6 else max(2 * heights - 1, 0))


def bit_of(dev_ref, height):
    return (dev_ref[0] >> height) & 1


def level_body(k, dev_ref, own, got, up_top_ref, out, *rest):
    hold = rest[-1]
    bit = bit_of(dev_ref, k)
    carry_at, coeff_at = (CARRY_AT, COEFF_AT) if k == 0 else (0, fixed_tiles(k) - 1)
    hold[bit, 0] = own[coeff_at]
    hold[1 - bit, 0] = got[coeff_at]
    pair = join(hold[0, 0], hold[1, 0])
    heights = range(lowest(k), k)
    for height in heights:
        hold[bit, 1 + height] = own[first_at(height, k)]
        hold[1 - bit, 1 + height] = got[first_at(height, k)]
        hold[bit, 7 + height] = own[last_at(height, k)]
        hold[1 - bit, 7 + height] = got[last_at(height, k)]
    if k < 5:
        parent = fused_halves(own[carry_at].astype(f32) + got[carry_at].astype(f32))
        if k < 4:
            out[0] = split(wide_dot(parent, split(up_top_ref[0, k + 1])))
        out[fixed_tiles(k + 1) - 1] = twice(parent).astype(bf16)
    if k == 2:
        side_out = rest[0]
        upper = bit_of(dev_ref, 3)
        for height in heights:
            hold[0, 7 + height] = hold[1, 7 + height]
            hold[1, 7 + height] = hold[0, 1 + height]
            out[fixed_tiles(3) + height] = hold[upper, 7 + height]
            side_out[height] = hold[1 - upper, 7 + height]
        out[fixed_tiles(3) + k] = pair
        side_out[k] = pair
    elif k < 5:
        for height in heights:
            out[first_at(height, k + 1)] = hold[0, 1 + height]
            out[last_at(height, k + 1)] = hold[1, 7 + height]
        out[first_at(k, k + 1)] = pair
    else:
        upper = bit_of(dev_ref, 6)
        for height in heights:
            hold[0, 7 + height] = hold[1, 7 + height]
            hold[1, 7 + height] = hold[0, 1 + height]
            out[first_at(height, 6)] = hold[upper, 7 + height]
        out[first_at(k, 6)] = pair


def level_call(k, dev, own, got, up_top):
    outs = [shape((tiles_of(k + 1), 64, 128), bf16)]
    if k == 2:
        outs += [shape((3, 64, 128), bf16)]
    ins = [own, got, up_top]
    return call(
        functools.partial(level_body, k),
        outs,
        scalars() + held(*ins),
        held(*outs),
        [pltpu.VMEM((2, 13, 64, 128), bf16)],
        name="level_%d" % k,
    )(dev, *ins)


def prepare_body(dev_ref, couple_ref, down_ref, couple_out, down_out):
    for height in range(6):
        odd = bit_of(dev_ref, height)
        even = 1 - odd
        picks = ((even, None), (1, odd), (2, even), (2 + even, None))
        for at, (slot, live) in enumerate(picks):
            matrix = couple_ref[0, height, slot]
            if live is not None:
                matrix = jnp.where(jnp.full(matrix.shape, live, jnp.int32) > 0, matrix, 0.0)
            couple_out[height, 64 * at : 64 * at + 64, :] = split(matrix)
    for height in range(5):
        down_out[height] = split(down_ref[0, height])


def prepare(dev, couple_top, down_top):
    outs = [shape((6, 256, 128), bf16), shape((5, 64, 128), bf16)]
    return call(
        prepare_body,
        outs,
        scalars() + held(couple_top, down_top),
        held(*outs),
        name="prepare",
    )(dev, couple_top, down_top)


def sides(dev_ref):
    odd = bit_of(dev_ref, 0)
    return 1 - odd, odd


def near_body(first, count, edges, devices, dev_ref, rhs_ref, points_ref, *rest):
    out_ref, kernels, rim_rhs, rim_source, rim_target = rest[-5:]
    leaves = rhs_ref.shape[0]

    def kernel_of(source, target):
        return lax.rsqrt(dot_columns(source, target)).astype(bf16)

    known = {}

    def rows(s):
        if s not in known:
            if s // 8 not in known.setdefault("groups", {}):
                known["groups"][s // 8] = Coordinates(points_ref, s // 8)
            known[s] = known["groups"][s // 8].rows(s % 8)
        return known[s]

    def build(s):
        source, target = rows(s)
        if s + 1 < leaves:
            targets = jnp.concatenate([target, rows(s + 1)[1]], axis=1)
            kernels[s % 2] = kernel_of(source, targets)
        else:
            kernels[s % 2, :, :256] = kernel_of(source, target)

    if edges:
        inner_ref, outer_ref = rest[:2]
        inner_at, outer_at = sides(dev_ref)
        rim_rhs[...] = jnp.zeros(rim_rhs.shape, bf16)
        rim_source[...] = rows(0)[0]
        rim_target[...] = rows(leaves - 1)[1]
        for halo, side in ((inner_ref, inner_at), (outer_ref, outer_at)):

            @pl.when((side == 0) & (dev_ref[0] > 0))
            def _():
                rim_rhs[0, :, :128] = halo[RHS_AT]
                rim_rhs[0, :, 128:] = halo[RHS_AT + 1]
                rim_source[:, :128] = halo[COORD_AT, 0:16, :]
                rim_source[:, 128:] = halo[COORD_AT, 16:32, :]

            @pl.when((side == 1) & (dev_ref[0] < devices - 1))
            def _():
                rim_rhs[1, :, :128] = halo[RHS_AT]
                rim_rhs[1, :, 128:] = halo[RHS_AT + 1]
                rim_target[:, :128] = halo[COORD_AT, 32:48, :]
                rim_target[:, 128:] = halo[COORD_AT, 48:64, :]

    build(first)
    for s in range(first, first + count):
        if s + 1 < first + count:
            build(s + 1)
        kernel = kernels[s % 2]
        own = dot(rhs_ref[s], kernel[:, :256])
        if s + 1 < leaves:
            own += dot_rows(rhs_ref[s + 1], kernel[:, 256:])
            out_ref[s + 1] = dot(rhs_ref[s], kernel[:, 256:])
        out_ref[s] = own if s == 0 else out_ref[s] + own

    if edges:
        before = kernel_of(rim_source[...], rows(0)[1])
        after = kernel_of(rows(leaves - 1)[0], rim_target[...])
        out_ref[0] += dot(rim_rhs[0], before)
        out_ref[leaves - 1] += dot_rows(rim_rhs[1], after)


def near(dev, rhs, points, first, count, halos, total):
    args = [rhs, points] + halos
    out = shape(rhs.shape, f32)
    aliases = {}
    if total is not None:
        aliases = {len(args) + 1: 0}
        args.append(total)
    return call(
        functools.partial(near_body, first, count, len(halos) > 0, lax.axis_size("leaf")),
        out,
        scalars() + held(*args),
        held(out)[0],
        [
            pltpu.VMEM((2, 256, 512), bf16),
            pltpu.VMEM((2, 64, 256), bf16),
            pltpu.VMEM((16, 256), bf16),
            pltpu.VMEM((16, 256), bf16),
        ],
        name="near_%d" % first,
        aliases=aliases,
    )(dev, *args)


def couple_body(
    dev_ref, list_ref, count_ref, node_list_ref, node_count_ref, leaf_ref, node_ref, inner_ref,
    outer_ref, blocks_ref, node_blocks_ref, gain_ref, node_gain_ref, leaf_hold, node_hold,
):
    leaves = leaf_ref.shape[0]
    groups = node_ref.shape[0]
    low = low_lanes((64, 128))

    def keep(hold, at, doubled):
        doubled = doubled.astype(f32)
        hold[0, at] = jnp.where(low, doubled, 0.0).astype(bf16)
        hold[1, at] = jnp.where(low, 0.0, doubled).astype(bf16)

    for leaf in range(leaves):
        keep(leaf_hold, W0 + leaf, leaf_ref[leaf])
    for node in range(groups):
        keep(node_hold, W1 + node, node_ref[node])
    nothing = jnp.zeros((64, 128), f32)
    keep(leaf_hold, leaves + 2 * W0, nothing)
    keep(node_hold, groups + 2 * W1, nothing)
    inner_side, outer_side = sides(dev_ref)
    for halo, side in ((inner_ref, inner_side), (outer_ref, outer_side)):

        def unpack(hold, at, tile):
            pair = halo[tile].astype(f32)
            turned = pltpu.roll(pair, 64, 1)
            keep(hold, at, jnp.where(low, pair, turned))
            keep(hold, at + 1, jnp.where(low, turned, pair))

        for j in range(4):
            unpack(leaf_hold, side * (leaves + W0) + 2 * j, LEAF_AT + j)
        for j in range(2):
            unpack(node_hold, side * (groups + W1) + 2 * j, NODE_AT + j)

    def picked(hold, lists, counts, row, first, slots, nothing):
        count = counts[row]
        at = [jnp.where(k < count, lists[k, row] - first, nothing) for k in range(slots)]
        return jnp.concatenate(
            [hold[0, at[2 * j]] + hold[1, at[2 * j + 1]] for j in range(slots // 2)], axis=1
        )

    def group(g, _):
        for b in range(8):
            row = g * 8 + b
            values = picked(
                leaf_hold, list_ref, count_ref, row, dev_ref[0] * leaves - W0, 8, leaves + 2 * W0
            )
            gain_ref[row] = dot(values, blocks_ref[row].reshape(512, 64))
        values = picked(
            node_hold, node_list_ref, node_count_ref, g, dev_ref[0] * groups - W1, 4, groups + 2 * W1
        )
        node_gain_ref[g] = dot(values, node_blocks_ref[g].reshape(256, 64))
        return 0

    for g in range(groups):
        group(g, 0)


def couple(dev, lists, counts, node_lists, node_counts, leaf, node, inner, outer, blocks, node_blocks):
    leaves, groups = leaf.shape[0], node.shape[0]
    outs = [shape((leaves, 64, 64), f32), shape((groups, 64, 64), f32)]
    ins = [leaf, node, inner, outer, blocks, node_blocks]
    return call(
        couple_body,
        outs,
        scalars(5) + held(*ins),
        held(*outs),
        [
            pltpu.VMEM((2, leaves + 2 * W0 + 1, 64, 128), bf16),
            pltpu.VMEM((2, groups + 2 * W1 + 1, 64, 128), bf16),
        ],
        name="couple",
    )(dev, lists, counts, node_lists, node_counts, *ins)


def downward_body(
    devices, dev_ref, side_ref, got_1, got_2, got_3, got_4, got_5, got_6, couple_ref, down_ref,
    down_node_ref, node_gain_ref, gain_ref, transfer_ref, bases_ref, sum_ref, out_ref, bank, out, sems,
):
    d = dev_ref[0]
    bank[0] = jnp.zeros((64, 128), bf16)
    for height in range(3):
        upper = bit_of(dev_ref, 3)
        bank[4 - 3 * upper + height] = got_3[fixed_tiles(3) + height]
        bank[1 + 3 * upper + height] = side_ref[height]
    start = {}
    at = 7
    for k, got in ((1, got_1), (2, got_2), (4, got_4), (5, got_5), (6, got_6)):
        start[k] = at - fixed_tiles(k)
        for tile in range(fixed_tiles(k), got.shape[0]):
            bank[at] = got[tile]
            at += 1
    gains = []
    for height in range(6):
        own = d >> (height + 1)
        left = right = 0
        if height < 3:
            left = jnp.where(d >= 8, 1 + height, 0)
            right = jnp.where(d < devices - 8, 4 + height, 0)
        for k in range(2 if height < 3 else 6, height, -1):
            bit = (own >> (k - height - 1)) & 1
            left = jnp.where(bit == 1, start[k] + last_at(height, k), left)
            right = jnp.where(bit == 0, start[k] + first_at(height, k), right)
        tiles = jnp.concatenate([bank[left], bank[right]], axis=1)
        gains.append(fused_halves(dot(tiles, couple_ref[height])))
    value = gains[5]
    for height in range(4, -1, -1):
        value = gains[height] + wide_dot(value, down_ref[height])
    rounded = value.astype(bf16)
    groups = down_node_ref.shape[0]

    def move(g):
        at = pl.ds(g * 8, 8)
        return pltpu.make_async_copy(out.at[at], out_ref.at[at], sems.at[g])

    node_values = [(node_gain_ref[g] + dot(rounded, down_node_ref[g])).astype(bf16) for g in range(groups)]
    for g in range(groups):
        bank[g, :, :64] = node_values[g]

    def group(g, _):
        node_value = bank[g, :, :64]
        leaf_values = [
            (gain_ref[g * 8 + b] + dot(node_value, transfer_ref[g * 8 + b])).astype(bf16) for b in range(8)
        ]
        for b in range(8):
            leaf = g * 8 + b
            out[leaf] = (sum_ref[leaf] + dot(leaf_values[b], bases_ref[leaf])).astype(bf16)
        move(g).start()
        return 0

    for g in range(groups):
        group(g, 0)
    for g in range(groups):
        move(g).wait()


def downward(dev, received, couple_parts, down_parts, down_node, node_gain, gain, transfer, bases, near_sum):
    ins = list(received) + [couple_parts, down_parts, down_node, node_gain, gain, transfer, bases, near_sum]
    out = shape(bases.shape, bf16)
    return call(
        functools.partial(downward_body, lax.axis_size("leaf")),
        out,
        scalars() + held(*ins),
        stored(out)[0],
        [
            pltpu.VMEM((7 + sum(tiles_of(k) - fixed_tiles(k) for k in range(1, 7)), 64, 128), bf16),
            pltpu.VMEM(out.shape, bf16),
            pltpu.SemaphoreType.DMA((down_node.shape[0],)),
        ],
        name="downward",
    )(dev, *ins)


def tied(*values):
    return lax.optimization_barrier(values)


def shards(
    rhs, points, upward_leaf_bases, downward_leaf_bases, up_leaf, leaf_down_transfer, couple_leaf,
    list_leaf, count_leaf, up_node, down_node, couple_node, list_node, count_node, up_top, down_top,
    couple_top,
):
    device = lax.axis_index("leaf")
    devices = lax.axis_size("leaf")
    dev = device.astype(jnp.int32).reshape(1)

    def beside(block, size):
        def partner(i):
            other = i + size if i // size % 2 == 1 else i - size
            return other if 0 <= other < devices else i

        return lax.ppermute(block, "leaf", [(i, partner(i)) for i in range(devices)])

    def exchange(block, mask):
        return lax.ppermute(block, "leaf", [(i, i ^ mask) for i in range(devices)])

    points = jnp.transpose(points, (1, 0, 2))
    leaf, node, inner_out, outer_out = upward(
        dev, rhs, points, upward_leaf_bases, up_leaf, up_node, up_top
    )
    inner = exchange(inner_out, 1)
    outer = beside(outer_out, 1)
    near_sum = near(dev, rhs, points, 0, parts[0], [], None)
    done = parts[0]
    own, got = inner_out, inner
    received = []
    for k in range(6):
        if k == 1:
            got, outer, near_sum = tied(got, outer, near_sum)
        else:
            got, near_sum = tied(got, near_sum)
        own, *edges = level_call(k, dev, own, got, up_top)
        got = exchange(own, PARTNERS[k])
        if k == 2:
            side = beside(edges[0], 8)
        received.append(got)
        near_sum, leaf, own = tied(near_sum, leaf, own)
        if k < 5:
            near_sum = near(
                dev, rhs, points, done, parts[k + 1], [inner, outer] if k == 4 else [], near_sum
            )
            done += parts[k + 1]
        if k == 3:
            side, near_sum = tied(side, near_sum)
    gain, node_gain = couple(
        dev, list_leaf.T, count_leaf, list_node.T, count_node, leaf, node, inner, outer,
        couple_leaf, couple_node,
    )
    couple_top, _ = tied(couple_top, own)
    couple_parts, down_parts = prepare(dev, couple_top, down_top)
    received[5], gain, couple_parts = tied(received[5], gain, couple_parts)
    return downward(
        dev, [side] + received, couple_parts, down_parts,
        down_node, node_gain, gain, leaf_down_transfer, downward_leaf_bases, near_sum,
    )


parts = (10, 12, 14, 8, 10, 10)


def solution(mesh):
    placed = tuple(P("leaf") for _ in range(17))
    return jax.shard_map(
        shards, mesh=mesh, in_specs=placed, out_specs=P("leaf"), check_vma=False
    )
```

```python
import functools

import jax
import jax.numpy as jnp
from jax import lax
from jax.experimental import pallas as pl
from jax.experimental.pallas import tpu as pltpu
from jax.sharding import PartitionSpec as P

bf16 = jnp.bfloat16
f32 = jnp.float32
core_square = 0.0004
W0 = 8
W1 = 4
LEAF_AT, NODE_AT, RHS_AT, COORD_AT, HALO_TILES = 0, 4, 6, 8, 9
CARRY_AT, COEFF_AT = 9, 10
CHUNKS = 4
PARTNERS = (2, 6, 8, 24)


def dot(a, b):
    return jnp.dot(a, b, preferred_element_type=f32)


def dot_rows(a, b):
    return lax.dot_general(a, b, (((1,), (1,)), ((), ())), preferred_element_type=f32)


def dot_columns(a, b):
    return lax.dot_general(a, b, (((0,), (0,)), ((), ())), preferred_element_type=f32)


def low_lanes(shape):
    return lax.broadcasted_iota(jnp.int32, shape, len(shape) - 1) < shape[-1] // 2


def join(low, high):
    return jnp.where(low_lanes(low.shape), low.astype(f32), high.astype(f32)).astype(bf16)


def twice(block):
    return jnp.concatenate([block, block], axis=1)


def split(wide):
    hi = wide.astype(bf16).astype(f32)
    return jnp.concatenate([hi, wide - hi], axis=1).astype(bf16)


def fused_halves(block):
    half = block.shape[1] // 2
    return block[:, :half] + block[:, half:]


def wide_dot(left, matrix_parts):
    weights = jnp.concatenate([matrix_parts, matrix_parts], axis=0)
    return fused_halves(dot(split(left), weights))


def call(body, out_shape, in_specs, out_specs, scratch=(), name=None, aliases=None, mib=24):
    return pl.pallas_call(
        body,
        out_shape=out_shape,
        in_specs=in_specs,
        out_specs=out_specs,
        scratch_shapes=list(scratch),
        input_output_aliases=aliases or {},
        compiler_params=pltpu.CompilerParams(vmem_limit_bytes=mib * 2**20),
        name=name,
    )


def held(*arrays):
    return [pl.BlockSpec(memory_space=pltpu.VMEM) for _ in arrays]


def stored(*arrays):
    return [pl.BlockSpec(memory_space=pltpu.HBM) for _ in arrays]


def scalars(count=1):
    return [pl.BlockSpec(memory_space=pltpu.SMEM)] * count


def shape(dims, dtype):
    return jax.ShapeDtypeStruct(dims, dtype)


def three_parts(value):
    hi = value.astype(bf16).astype(f32)
    mid = (value - hi).astype(bf16).astype(f32)
    return hi, mid, value - hi - mid


class Coordinates:
    def __init__(self, points, group):
        self.scaled = [points[j, group * 8 : group * 8 + 8, :].astype(f32) * 256.0 for j in range(3)]
        square = sum(x * x for x in self.scaled)
        self.parts = three_parts(square)
        self.plus_core = three_parts(square + core_square * 65536.0)

    def rows(self, b):
        row = lax.broadcasted_iota(jnp.int32, (16, self.scaled[0].shape[1]), 0)

        def stacked(values, ones_at):
            rows = jnp.where((row >= ones_at) & (row < ones_at + 3), 1.0, 0.0)
            for at, value in values:
                rows = jnp.where(row == at, value[b : b + 1], rows)
            return rows.astype(bf16)

        source = stacked(
            [(j, -2.0 * self.scaled[j]) for j in range(3)] + [(6 + j, self.plus_core[j]) for j in range(3)], 3
        )
        target = stacked(
            [(j, self.scaled[j]) for j in range(3)] + [(3 + j, self.parts[j]) for j in range(3)], 6
        )
        return source, target


def upward_body(
    dev_ref, rhs_ref, points_ref, bases_ref, up_leaf_ref, up_node_ref, up_top_ref,
    leaf_ref, node_ref, inner_ref, outer_ref,
    rhs, bases, up_leaf, points, up_node, up_top, sems, more_sems,
):
    groups = up_node_ref.shape[0]
    odd = lax.rem(dev_ref[0], 2) == 1

    leaves = rhs_ref.shape[0]
    chunk = leaves // CHUNKS

    def moves(c):
        at = pl.ds(c * chunk, chunk)
        return [
            pltpu.make_async_copy(rhs_ref.at[at], rhs.at[at], sems.at[0, c]),
            pltpu.make_async_copy(bases_ref.at[at], bases.at[at], sems.at[1, c]),
        ]

    others = [
        pltpu.make_async_copy(points_ref, points, more_sems.at[0]),
        pltpu.make_async_copy(up_node_ref, up_node, more_sems.at[1]),
        pltpu.make_async_copy(up_top_ref.at[0, 0], up_top, more_sems.at[2]),
        pltpu.make_async_copy(up_leaf_ref, up_leaf, more_sems.at[3]),
    ]
    others[0].start()
    for c in range(CHUNKS):
        for move in moves(c):
            move.start()
        if c == 0:
            others[3].start()
    others[1].start()
    others[2].start()
    for c in range(CHUNKS):
        for move in moves(c):
            move.wait()
        for leaf in range(c * chunk, (c + 1) * chunk):
            base = bases[leaf]
            leaf_ref[leaf] = dot_rows(rhs[leaf], jnp.concatenate([base, base], axis=0)).astype(bf16)

    others[3].wait()
    others[1].wait()
    nodes = []
    for g in range(groups):
        pairs = [join(leaf_ref[g * 8 + 2 * j], leaf_ref[g * 8 + 2 * j + 1]) for j in range(4)]
        up = up_leaf[g * 8 : g * 8 + 8].reshape(512, 64)
        nodes.append(twice(dot(jnp.concatenate(pairs, axis=1), up)).astype(bf16))
        node_ref[g] = nodes[g]
    pairs = [join(nodes[2 * j], nodes[2 * j + 1]) for j in range(groups // 2)]
    coeff = dot(jnp.concatenate(pairs, axis=1), up_node[...].reshape(groups * 64, 64))
    others[0].wait()
    others[2].wait()
    inner_ref[CARRY_AT] = split(wide_dot(coeff, split(up_top[...])))
    inner_ref[COEFF_AT] = twice(coeff).astype(bf16)

    def edge(message, first_leaf, leaf, first_node):
        for j in range(4):
            message[LEAF_AT + j] = join(leaf_ref[first_leaf + 2 * j], leaf_ref[first_leaf + 2 * j + 1])
        for j in range(2):
            message[NODE_AT + j] = join(node_ref[first_node + 2 * j], node_ref[first_node + 2 * j + 1])
        message[RHS_AT] = rhs[leaf, :, :128]
        message[RHS_AT + 1] = rhs[leaf, :, 128:]
        source, target = Coordinates(points, leaf // 8).rows(leaf % 8)
        message[COORD_AT, 0:16, :] = source[:, :128]
        message[COORD_AT, 16:32, :] = source[:, 128:]
        message[COORD_AT, 32:48, :] = target[:, :128]
        message[COORD_AT, 48:64, :] = target[:, 128:]

    @pl.when(odd)
    def _():
        edge(inner_ref, 0, 0, 0)
        edge(outer_ref, leaves - W0, leaves - 1, groups - W1)

    @pl.when(~odd)
    def _():
        edge(outer_ref, 0, 0, 0)
        edge(inner_ref, leaves - W0, leaves - 1, groups - W1)


def upward(dev, rhs, points, bases, up_leaf, up_node, up_top):
    leaves = rhs.shape[0]
    groups = up_node.shape[0]
    outs = [
        shape((leaves, 64, 128), bf16),
        shape((groups, 64, 128), bf16),
        shape((HALO_TILES + 2, 64, 128), bf16),
        shape((HALO_TILES, 64, 128), bf16),
    ]
    ins = [rhs, points, bases, up_leaf, up_node, up_top]
    return call(
        upward_body,
        outs,
        scalars() + stored(*ins),
        held(*outs),
        [
            pltpu.VMEM(rhs.shape, bf16),
            pltpu.VMEM(bases.shape, bf16),
            pltpu.VMEM(up_leaf.shape, bf16),
            pltpu.VMEM(points.shape, bf16),
            pltpu.VMEM(up_node.shape, bf16),
            pltpu.VMEM((64, 64), f32),
            pltpu.SemaphoreType.DMA((2, CHUNKS)),
            pltpu.SemaphoreType.DMA((4,)),
        ],
        name="upward",
        mib=56,
    )(dev, *ins)


TILES = {1: 3, 2: 5, 3: 5, 4: 3}
CARRY, COEFF, PAIR = 0, 1, 2
FIRST, LAST, PARENT_PAIR = 2, 3, 4


def bit_of(dev_ref, height):
    return (dev_ref[0] >> height) & 1


def in_order(own, got, bit, hold):
    hold[bit] = own
    hold[1 - bit] = got
    return hold[0], hold[1]


def level_body(k, dev_ref, own, got, up_top_ref, out, *rest):
    hold = rest[-1]
    bit = bit_of(dev_ref, k)
    carry_at, coeff_at = (CARRY_AT, COEFF_AT) if k == 0 else (CARRY, COEFF)
    pair = join(*in_order(own[coeff_at], got[coeff_at], bit, hold))
    parent = fused_halves(own[carry_at].astype(f32) + got[carry_at].astype(f32))
    coeff = twice(parent).astype(bf16)
    if k < 4:
        out[CARRY] = split(wide_dot(parent, split(up_top_ref[0, k + 1])))
        out[COEFF] = coeff
    if k == 0 or k == 3:
        out[PAIR] = pair
    elif k == 1:
        out[FIRST], out[LAST] = in_order(own[PAIR], got[PAIR], bit, hold)
        out[PARENT_PAIR] = pair
    elif k == 2:
        side_out = rest[0]
        upper = bit_of(dev_ref, 3)
        first = in_order(own[FIRST], got[FIRST], bit, hold)[0]
        last = in_order(own[LAST], got[LAST], bit, hold)[1]
        out[2], side_out[0] = in_order(last, first, upper, hold)
        first, last = in_order(own[PARENT_PAIR], got[PARENT_PAIR], bit, hold)
        out[3], side_out[1] = in_order(last, first, upper, hold)
        out[4] = pair
        side_out[2] = pair
    else:
        far_out, across_out = rest[:2]
        first, last = in_order(own[PAIR], got[PAIR], bit, hold)
        out[0], far_out[0] = in_order(last, first, bit_of(dev_ref, 5), hold)
        out[1] = pair
        far_out[1] = pair
        far_out[2] = coeff
        across_out[0] = coeff


def level_call(k, dev, own, got, up_top):
    tiles = {2: (TILES[3], 3), 4: (2, 3, 1)}.get(k) or (TILES[k + 1],)
    outs = [shape((count, 64, 128), bf16) for count in tiles]
    ins = [own, got, up_top]
    return call(
        functools.partial(level_body, k),
        outs,
        scalars() + held(*ins),
        held(*outs),
        [pltpu.VMEM((2, 64, 128), bf16)],
        name="level_%d" % k,
    )(dev, *ins)


def prepare_body(dev_ref, couple_ref, down_ref, couple_out, down_out):
    for height in range(6):
        odd = bit_of(dev_ref, height)
        even = 1 - odd
        picks = ((even, None), (1, odd), (2, even), (2 + even, None))
        for at, (slot, live) in enumerate(picks):
            matrix = couple_ref[0, height, slot]
            if live is not None:
                matrix = jnp.where(jnp.full(matrix.shape, live, jnp.int32) > 0, matrix, 0.0)
            couple_out[height, 64 * at : 64 * at + 64, :] = split(matrix)
    for height in range(5):
        down_out[height] = split(down_ref[0, height])


def prepare(dev, couple_top, down_top):
    outs = [shape((6, 256, 128), bf16), shape((5, 64, 128), bf16)]
    return call(
        prepare_body,
        outs,
        scalars() + held(couple_top, down_top),
        held(*outs),
        name="prepare",
    )(dev, couple_top, down_top)


def sides(dev_ref):
    odd = bit_of(dev_ref, 0)
    return 1 - odd, odd


def near_body(first, count, edges, devices, dev_ref, rhs_ref, points_ref, *rest):
    out_ref, kernels, rim_rhs, rim_source, rim_target = rest[-5:]
    leaves = rhs_ref.shape[0]

    def kernel_of(source, target):
        return lax.rsqrt(dot_columns(source, target)).astype(bf16)

    known = {}

    def rows(s):
        if s not in known:
            if s // 8 not in known.setdefault("groups", {}):
                known["groups"][s // 8] = Coordinates(points_ref, s // 8)
            known[s] = known["groups"][s // 8].rows(s % 8)
        return known[s]

    def build(s):
        source, target = rows(s)
        if s + 1 < leaves:
            targets = jnp.concatenate([target, rows(s + 1)[1]], axis=1)
            kernels[s % 2] = kernel_of(source, targets)
        else:
            kernels[s % 2, :, :256] = kernel_of(source, target)

    if edges:
        inner_ref, outer_ref = rest[:2]
        inner_at, outer_at = sides(dev_ref)
        rim_rhs[...] = jnp.zeros(rim_rhs.shape, bf16)
        rim_source[...] = rows(0)[0]
        rim_target[...] = rows(leaves - 1)[1]
        for halo, side in ((inner_ref, inner_at), (outer_ref, outer_at)):

            @pl.when((side == 0) & (dev_ref[0] > 0))
            def _():
                rim_rhs[0, :, :128] = halo[RHS_AT]
                rim_rhs[0, :, 128:] = halo[RHS_AT + 1]
                rim_source[:, :128] = halo[COORD_AT, 0:16, :]
                rim_source[:, 128:] = halo[COORD_AT, 16:32, :]

            @pl.when((side == 1) & (dev_ref[0] < devices - 1))
            def _():
                rim_rhs[1, :, :128] = halo[RHS_AT]
                rim_rhs[1, :, 128:] = halo[RHS_AT + 1]
                rim_target[:, :128] = halo[COORD_AT, 32:48, :]
                rim_target[:, 128:] = halo[COORD_AT, 48:64, :]

    if count > 0:
        build(first)
    for s in range(first, first + count):
        if s + 1 < first + count:
            build(s + 1)
        kernel = kernels[s % 2]
        own = dot(rhs_ref[s], kernel[:, :256])
        if s + 1 < leaves:
            own += dot_rows(rhs_ref[s + 1], kernel[:, 256:])
            out_ref[s + 1] = dot(rhs_ref[s], kernel[:, 256:])
        out_ref[s] = own if s == 0 else out_ref[s] + own

    if edges:
        before = kernel_of(rim_source[...], rows(0)[1])
        after = kernel_of(rows(leaves - 1)[0], rim_target[...])
        out_ref[0] += dot(rim_rhs[0], before)
        out_ref[leaves - 1] += dot_rows(rim_rhs[1], after)


def near(dev, rhs, points, first, count, halos, total):
    args = [rhs, points] + halos
    out = shape(rhs.shape, f32)
    aliases = {}
    if total is not None:
        aliases = {len(args) + 1: 0}
        args.append(total)
    return call(
        functools.partial(near_body, first, count, len(halos) > 0, lax.axis_size("leaf")),
        out,
        scalars() + held(*args),
        held(out)[0],
        [
            pltpu.VMEM((2, 256, 512), bf16),
            pltpu.VMEM((2, 64, 256), bf16),
            pltpu.VMEM((16, 256), bf16),
            pltpu.VMEM((16, 256), bf16),
        ],
        name="near_%d" % first,
        aliases=aliases,
    )(dev, *args)


def couple_body(
    dev_ref, list_ref, count_ref, node_list_ref, node_count_ref, leaf_ref, node_ref, inner_ref,
    outer_ref, blocks_ref, node_blocks_ref, gain_ref, node_gain_ref, leaf_hold, node_hold,
):
    leaves = leaf_ref.shape[0]
    groups = node_ref.shape[0]
    low = low_lanes((64, 128))

    def keep(hold, at, doubled):
        doubled = doubled.astype(f32)
        hold[0, at] = jnp.where(low, doubled, 0.0).astype(bf16)
        hold[1, at] = jnp.where(low, 0.0, doubled).astype(bf16)

    for leaf in range(leaves):
        keep(leaf_hold, W0 + leaf, leaf_ref[leaf])
    for node in range(groups):
        keep(node_hold, W1 + node, node_ref[node])
    nothing = jnp.zeros((64, 128), f32)
    keep(leaf_hold, leaves + 2 * W0, nothing)
    keep(node_hold, groups + 2 * W1, nothing)
    inner_side, outer_side = sides(dev_ref)
    for halo, side in ((inner_ref, inner_side), (outer_ref, outer_side)):

        def unpack(hold, at, tile):
            pair = halo[tile].astype(f32)
            turned = pltpu.roll(pair, 64, 1)
            keep(hold, at, jnp.where(low, pair, turned))
            keep(hold, at + 1, jnp.where(low, turned, pair))

        for j in range(4):
            unpack(leaf_hold, side * (leaves + W0) + 2 * j, LEAF_AT + j)
        for j in range(2):
            unpack(node_hold, side * (groups + W1) + 2 * j, NODE_AT + j)

    def picked(hold, lists, counts, row, first, slots, nothing):
        count = counts[row]
        at = [jnp.where(k < count, lists[k, row] - first, nothing) for k in range(slots)]
        return jnp.concatenate(
            [hold[0, at[2 * j]] + hold[1, at[2 * j + 1]] for j in range(slots // 2)], axis=1
        )

    def group(g, _):
        for b in range(8):
            row = g * 8 + b
            values = picked(
                leaf_hold, list_ref, count_ref, row, dev_ref[0] * leaves - W0, 8, leaves + 2 * W0
            )
            gain_ref[row] = dot(values, blocks_ref[row].reshape(512, 64))
        values = picked(
            node_hold, node_list_ref, node_count_ref, g, dev_ref[0] * groups - W1, 4, groups + 2 * W1
        )
        node_gain_ref[g] = dot(values, node_blocks_ref[g].reshape(256, 64))
        return 0

    for g in range(groups):
        group(g, 0)


def couple(dev, lists, counts, node_lists, node_counts, leaf, node, inner, outer, blocks, node_blocks):
    leaves, groups = leaf.shape[0], node.shape[0]
    outs = [shape((leaves, 64, 64), f32), shape((groups, 64, 64), f32)]
    ins = [leaf, node, inner, outer, blocks, node_blocks]
    return call(
        couple_body,
        outs,
        scalars(5) + held(*ins),
        held(*outs),
        [
            pltpu.VMEM((2, leaves + 2 * W0 + 1, 64, 128), bf16),
            pltpu.VMEM((2, groups + 2 * W1 + 1, 64, 128), bf16),
        ],
        name="couple",
    )(dev, lists, counts, node_lists, node_counts, *ins)


def downward_body(
    devices, dev_ref, side_ref, got_1, got_2, got_3, got_4, near_ref, far_ref, across_ref, couple_ref,
    down_ref, down_node_ref, node_gain_ref, gain_ref, transfer_ref, bases_ref, sum_ref, out_ref, bank,
    out, sems,
):
    d = dev_ref[0]
    pick = jnp.where
    bank[0] = jnp.zeros((64, 128), bf16)
    upper = bit_of(dev_ref, 3)
    for height in range(3):
        bank[4 - 3 * upper + height] = got_3[2 + height]
        bank[1 + 3 * upper + height] = side_ref[height]
    bank[7] = got_1[PAIR]
    bank[8] = got_2[FIRST]
    bank[9] = got_2[LAST]
    bank[10] = got_2[PARENT_PAIR]
    bank[11] = got_4[PAIR]
    bank[12] = near_ref[0]
    bank[13] = near_ref[1]
    bank[14] = far_ref[0]
    bank[15] = far_ref[1]
    group = d >> 5
    odd = group & 1
    bank[16 + odd] = across_ref[0]
    bank[17 - odd] = far_ref[2]
    bank[16] = join(bank[16], bank[17])
    before = [pick(d >= 8, 1 + height, 0) for height in range(3)]
    after = [pick(d < devices - 8, 4 + height, 0) for height in range(3)]
    parent = d >> 1
    even = (parent & 1) == 0
    left = [pick(even, pick((parent & 3) == 2, 9, before[0]), 7)]
    right = [pick(even, 7, pick((parent & 3) == 1, 8, after[0]))]
    even = ((d >> 2) & 1) == 0
    left += [pick(even, before[1], 10), before[2]]
    right += [pick(even, 10, after[1]), after[2]]
    even = ((d >> 4) & 1) == 0
    beside_left = [pick(odd == 1, 12 + j, pick(group == 2, 14 + j, 0)) for j in range(2)]
    beside_right = [pick(odd == 0, 12 + j, pick(group == 1, 14 + j, 0)) for j in range(2)]
    left += [pick(even, beside_left[0], 11), beside_left[1], pick(group >= 2, 16, 0)]
    right += [pick(even, 11, beside_right[0]), beside_right[1], pick(group >= 2, 0, 16)]
    gains = []
    for height in range(6):
        tiles = jnp.concatenate([bank[left[height]], bank[right[height]]], axis=1)
        gains.append(fused_halves(dot(tiles, couple_ref[height])))
    value = gains[5]
    for height in range(4, -1, -1):
        value = gains[height] + wide_dot(value, down_ref[height])
    rounded = value.astype(bf16)
    groups = down_node_ref.shape[0]

    def move(g):
        at = pl.ds(g * 8, 8)
        return pltpu.make_async_copy(out.at[at], out_ref.at[at], sems.at[g])

    node_values = [(node_gain_ref[g] + dot(rounded, down_node_ref[g])).astype(bf16) for g in range(groups)]
    for g in range(groups):
        bank[g, :, :64] = node_values[g]

    def group(g, _):
        node_value = bank[g, :, :64]
        leaf_values = [
            (gain_ref[g * 8 + b] + dot(node_value, transfer_ref[g * 8 + b])).astype(bf16) for b in range(8)
        ]
        for b in range(8):
            leaf = g * 8 + b
            out[leaf] = (sum_ref[leaf] + dot(leaf_values[b], bases_ref[leaf])).astype(bf16)
        move(g).start()
        return 0

    for g in range(groups):
        group(g, 0)
    for g in range(groups):
        move(g).wait()


def downward(dev, received, couple_parts, down_parts, down_node, node_gain, gain, transfer, bases, near_sum):
    ins = list(received) + [couple_parts, down_parts, down_node, node_gain, gain, transfer, bases, near_sum]
    out = shape(bases.shape, bf16)
    return call(
        functools.partial(downward_body, lax.axis_size("leaf")),
        out,
        scalars() + held(*ins),
        stored(out)[0],
        [
            pltpu.VMEM((18, 64, 128), bf16),
            pltpu.VMEM(out.shape, bf16),
            pltpu.SemaphoreType.DMA((down_node.shape[0],)),
        ],
        name="downward",
    )(dev, *ins)


def tied(*values):
    return lax.optimization_barrier(values)


def shards(
    rhs, points, upward_leaf_bases, downward_leaf_bases, up_leaf, leaf_down_transfer, couple_leaf,
    list_leaf, count_leaf, up_node, down_node, couple_node, list_node, count_node, up_top, down_top,
    couple_top,
):
    device = lax.axis_index("leaf")
    devices = lax.axis_size("leaf")
    dev = device.astype(jnp.int32).reshape(1)

    def beside(block, size):
        route = [(i, (i + size if i // size % 2 == 1 else i - size) % devices) for i in range(devices)]
        return lax.ppermute(block, "leaf", route)

    def exchange(block, mask):
        return lax.ppermute(block, "leaf", [(i, i ^ mask) for i in range(devices)])

    points = jnp.transpose(points, (1, 0, 2))
    leaf, node, inner_out, outer_out = upward(
        dev, rhs, points, upward_leaf_bases, up_leaf, up_node, up_top
    )
    got = inner = exchange(inner_out, 1)
    if OUTER_AFTER < 0:
        outer = beside(outer_out, 1)
    near_sum = near(dev, rhs, points, 0, PARTS[0], [], None)
    done = PARTS[0]
    own = inner_out
    received = []
    for k in range(4):
        got, near_sum = tied(got, near_sum)
        own, *edges = level_call(k, dev, own, got, up_top)
        got = exchange(own, PARTNERS[k])
        received.append(got)
        if k == 2:
            side_out = edges[0]
        if k == SIDE_AFTER:
            side_out, own = tied(side_out, own)
            side = beside(side_out, 8)
        if k == OUTER_AFTER:
            outer_out, own = tied(outer_out, own)
            outer = beside(outer_out, 1)
        near_sum, own = tied(near_sum, own)
        if PARTS[k + 1] > 0:
            near_sum = near(dev, rhs, points, done, PARTS[k + 1], [], near_sum)
            done += PARTS[k + 1]
        if k == COUPLE_AFTER:
            leaf, outer, own = tied(leaf, outer, own)
            gain, node_gain = couple(
                dev, list_leaf.T, count_leaf, list_node.T, count_node, leaf, node, inner, outer,
                couple_leaf, couple_node,
            )
            near_sum, gain = tied(near_sum, gain)
        if k == 2:
            couple_top, _ = tied(couple_top, own)
            couple_parts, down_parts = prepare(dev, couple_top, down_top)
            near_sum, couple_parts = tied(near_sum, couple_parts)
    got, near_sum, outer, side = tied(got, near_sum, outer, side)
    near_out, far_out, across_out = level_call(4, dev, own, got, up_top)
    last = [exchange(near_out, 32), exchange(far_out, 96), exchange(across_out, 64)]
    near_sum, near_out = tied(near_sum, near_out)
    near_sum = near(dev, rhs, points, done, PARTS[5], [inner, outer], near_sum)
    *last, near_sum = tied(*last, near_sum)
    return downward(
        dev, [side] + received + last, couple_parts, down_parts,
        down_node, node_gain, gain, leaf_down_transfer, downward_leaf_bases, near_sum,
    )


OUTER_AFTER = 0
COUPLE_AFTER = 3
SIDE_AFTER = 2
PARTS = (11, 14, 14, 12, 0, 13)


def solution(mesh):
    placed = tuple(P("leaf") for _ in range(17))
    return jax.shard_map(
        shards, mesh=mesh, in_specs=placed, out_specs=P("leaf"), check_vma=False
    )
```

```python
import functools

import jax
import jax.numpy as jnp
from jax import lax
from jax.experimental import pallas as pl
from jax.experimental.pallas import tpu as pltpu
from jax.sharding import PartitionSpec as P

bf16 = jnp.bfloat16
f32 = jnp.float32
core_square = 0.0004
W0 = 8
W1 = 4
LEAF_AT, NODE_AT, RHS_AT, COORD_AT, HALO_TILES = 0, 4, 6, 8, 9
CARRY_AT, COEFF_AT = 9, 10
CHUNKS = 4
PARTNERS = (2, 6, 8, 24)


def dot(a, b):
    return jnp.dot(a, b, preferred_element_type=f32)


def dot_rows(a, b):
    return lax.dot_general(a, b, (((1,), (1,)), ((), ())), preferred_element_type=f32)


def dot_columns(a, b):
    return lax.dot_general(a, b, (((0,), (0,)), ((), ())), preferred_element_type=f32)


def low_lanes(shape):
    return lax.broadcasted_iota(jnp.int32, shape, len(shape) - 1) < shape[-1] // 2


def join(low, high):
    return jnp.where(low_lanes(low.shape), low.astype(f32), high.astype(f32)).astype(bf16)


def twice(block):
    return jnp.concatenate([block, block], axis=1)


def split(wide):
    hi = wide.astype(bf16).astype(f32)
    return jnp.concatenate([hi, wide - hi], axis=1).astype(bf16)


def fused_halves(block):
    half = block.shape[1] // 2
    return block[:, :half] + block[:, half:]


def wide_dot(left, matrix_parts):
    weights = jnp.concatenate([matrix_parts, matrix_parts], axis=0)
    return fused_halves(dot(split(left), weights))


def call(body, out_shape, in_specs, out_specs, scratch=(), name=None, aliases=None, mib=24):
    return pl.pallas_call(
        body,
        out_shape=out_shape,
        in_specs=in_specs,
        out_specs=out_specs,
        scratch_shapes=list(scratch),
        input_output_aliases=aliases or {},
        compiler_params=pltpu.CompilerParams(vmem_limit_bytes=mib * 2**20),
        name=name,
    )


def held(*arrays):
    return [pl.BlockSpec(memory_space=pltpu.VMEM) for _ in arrays]


def stored(*arrays):
    return [pl.BlockSpec(memory_space=pltpu.HBM) for _ in arrays]


def scalars(count=1):
    return [pl.BlockSpec(memory_space=pltpu.SMEM)] * count


def shape(dims, dtype):
    return jax.ShapeDtypeStruct(dims, dtype)


def three_parts(value):
    hi = value.astype(bf16).astype(f32)
    mid = (value - hi).astype(bf16).astype(f32)
    return hi, mid, value - hi - mid


class Coordinates:
    def __init__(self, points, group):
        self.scaled = [points[j, group * 8 : group * 8 + 8, :].astype(f32) * 256.0 for j in range(3)]
        square = sum(x * x for x in self.scaled)
        self.parts = three_parts(square)
        self.plus_core = three_parts(square + core_square * 65536.0)

    def rows(self, b):
        row = lax.broadcasted_iota(jnp.int32, (16, self.scaled[0].shape[1]), 0)

        def stacked(values, ones_at):
            rows = jnp.where((row >= ones_at) & (row < ones_at + 3), 1.0, 0.0)
            for at, value in values:
                rows = jnp.where(row == at, value[b : b + 1], rows)
            return rows.astype(bf16)

        source = stacked(
            [(j, -2.0 * self.scaled[j]) for j in range(3)] + [(6 + j, self.plus_core[j]) for j in range(3)], 3
        )
        target = stacked(
            [(j, self.scaled[j]) for j in range(3)] + [(3 + j, self.parts[j]) for j in range(3)], 6
        )
        return source, target


def upward_body(
    dev_ref, rhs_ref, points_ref, bases_ref, up_leaf_ref, up_node_ref, up_top_ref,
    leaf_ref, node_ref, inner_ref, outer_ref,
    rhs, bases, up_leaf, points, up_node, up_top, sems, more_sems,
):
    groups = up_node_ref.shape[0]
    odd = lax.rem(dev_ref[0], 2) == 1

    leaves = rhs_ref.shape[0]
    chunk = leaves // CHUNKS

    def moves(c):
        at = pl.ds(c * chunk, chunk)
        return [
            pltpu.make_async_copy(rhs_ref.at[at], rhs.at[at], sems.at[0, c]),
            pltpu.make_async_copy(bases_ref.at[at], bases.at[at], sems.at[1, c]),
        ]

    others = [
        pltpu.make_async_copy(points_ref, points, more_sems.at[0]),
        pltpu.make_async_copy(up_node_ref, up_node, more_sems.at[1]),
        pltpu.make_async_copy(up_top_ref.at[0, 0], up_top, more_sems.at[2]),
        pltpu.make_async_copy(up_leaf_ref, up_leaf, more_sems.at[3]),
    ]
    others[0].start()
    for c in range(CHUNKS):
        for move in moves(c):
            move.start()
        if c == 0:
            others[3].start()
    others[1].start()
    others[2].start()
    for c in range(CHUNKS):
        for move in moves(c):
            move.wait()
        for leaf in range(c * chunk, (c + 1) * chunk):
            leaf_ref[leaf] = twice(dot_rows(rhs[leaf], bases[leaf])).astype(bf16)

    others[3].wait()
    others[1].wait()
    nodes = []
    for g in range(groups):
        pairs = [join(leaf_ref[g * 8 + 2 * j], leaf_ref[g * 8 + 2 * j + 1]) for j in range(4)]
        up = up_leaf[g * 8 : g * 8 + 8].reshape(512, 64)
        nodes.append(twice(dot(jnp.concatenate(pairs, axis=1), up)).astype(bf16))
        node_ref[g] = nodes[g]
    pairs = [join(nodes[2 * j], nodes[2 * j + 1]) for j in range(groups // 2)]
    coeff = dot(jnp.concatenate(pairs, axis=1), up_node[...].reshape(groups * 64, 64))
    others[0].wait()
    others[2].wait()
    inner_ref[CARRY_AT] = split(wide_dot(coeff, split(up_top[...])))
    inner_ref[COEFF_AT] = twice(coeff).astype(bf16)

    def edge(message, first_leaf, leaf, first_node):
        for j in range(4):
            message[LEAF_AT + j] = join(leaf_ref[first_leaf + 2 * j], leaf_ref[first_leaf + 2 * j + 1])
        for j in range(2):
            message[NODE_AT + j] = join(node_ref[first_node + 2 * j], node_ref[first_node + 2 * j + 1])
        message[RHS_AT] = rhs[leaf, :, :128]
        message[RHS_AT + 1] = rhs[leaf, :, 128:]
        source, target = Coordinates(points, leaf // 8).rows(leaf % 8)
        message[COORD_AT, 0:16, :] = source[:, :128]
        message[COORD_AT, 16:32, :] = source[:, 128:]
        message[COORD_AT, 32:48, :] = target[:, :128]
        message[COORD_AT, 48:64, :] = target[:, 128:]

    @pl.when(odd)
    def _():
        edge(inner_ref, 0, 0, 0)
        edge(outer_ref, leaves - W0, leaves - 1, groups - W1)

    @pl.when(~odd)
    def _():
        edge(outer_ref, 0, 0, 0)
        edge(inner_ref, leaves - W0, leaves - 1, groups - W1)


def upward(dev, rhs, points, bases, up_leaf, up_node, up_top):
    leaves = rhs.shape[0]
    groups = up_node.shape[0]
    outs = [
        shape((leaves, 64, 128), bf16),
        shape((groups, 64, 128), bf16),
        shape((HALO_TILES + 2, 64, 128), bf16),
        shape((HALO_TILES, 64, 128), bf16),
    ]
    ins = [rhs, points, bases, up_leaf, up_node, up_top]
    return call(
        upward_body,
        outs,
        scalars() + stored(*ins),
        held(*outs),
        [
            pltpu.VMEM(rhs.shape, bf16),
            pltpu.VMEM(bases.shape, bf16),
            pltpu.VMEM(up_leaf.shape, bf16),
            pltpu.VMEM(points.shape, bf16),
            pltpu.VMEM(up_node.shape, bf16),
            pltpu.VMEM((64, 64), f32),
            pltpu.SemaphoreType.DMA((2, CHUNKS)),
            pltpu.SemaphoreType.DMA((4,)),
        ],
        name="upward",
        mib=56,
    )(dev, *ins)


TILES = {1: 3, 2: 5, 3: 5, 4: 3}
CARRY, COEFF, PAIR = 0, 1, 2
FIRST, LAST, PARENT_PAIR = 2, 3, 4


def bit_of(dev_ref, height):
    return (dev_ref[0] >> height) & 1


def in_order(own, got, bit, hold):
    hold[bit] = own
    hold[1 - bit] = got
    return hold[0], hold[1]


def level_body(k, dev_ref, own, got, up_top_ref, out, *rest):
    hold = rest[-1]
    bit = bit_of(dev_ref, k)
    carry_at, coeff_at = (CARRY_AT, COEFF_AT) if k == 0 else (CARRY, COEFF)
    pair = join(*in_order(own[coeff_at], got[coeff_at], bit, hold))
    parent = fused_halves(own[carry_at].astype(f32) + got[carry_at].astype(f32))
    coeff = twice(parent).astype(bf16)
    if k < 4:
        out[CARRY] = split(wide_dot(parent, split(up_top_ref[0, k + 1])))
        out[COEFF] = coeff
    if k == 0 or k == 3:
        out[PAIR] = pair
    elif k == 1:
        out[FIRST], out[LAST] = in_order(own[PAIR], got[PAIR], bit, hold)
        out[PARENT_PAIR] = pair
    elif k == 2:
        side_out = rest[0]
        upper = bit_of(dev_ref, 3)
        first = in_order(own[FIRST], got[FIRST], bit, hold)[0]
        last = in_order(own[LAST], got[LAST], bit, hold)[1]
        out[2], side_out[0] = in_order(last, first, upper, hold)
        first, last = in_order(own[PARENT_PAIR], got[PARENT_PAIR], bit, hold)
        out[3], side_out[1] = in_order(last, first, upper, hold)
        out[4] = pair
        side_out[2] = pair
    else:
        far_out, across_out = rest[:2]
        first, last = in_order(own[PAIR], got[PAIR], bit, hold)
        out[0], far_out[0] = in_order(last, first, bit_of(dev_ref, 5), hold)
        out[1] = pair
        far_out[1] = pair
        far_out[2] = coeff
        across_out[0] = coeff


def level_call(k, dev, own, got, up_top):
    tiles = {2: (TILES[3], 3), 4: (2, 3, 1)}.get(k) or (TILES[k + 1],)
    outs = [shape((count, 64, 128), bf16) for count in tiles]
    ins = [own, got, up_top]
    return call(
        functools.partial(level_body, k),
        outs,
        scalars() + held(*ins),
        held(*outs),
        [pltpu.VMEM((2, 64, 128), bf16)],
        name="level_%d" % k,
    )(dev, *ins)


def prepare_body(dev_ref, couple_ref, down_ref, couple_out, down_out):
    for height in range(6):
        odd = bit_of(dev_ref, height)
        even = 1 - odd
        picks = ((even, None), (1, odd), (2, even), (2 + even, None))
        for at, (slot, live) in enumerate(picks):
            matrix = couple_ref[0, height, slot]
            if live is not None:
                matrix = jnp.where(jnp.full(matrix.shape, live, jnp.int32) > 0, matrix, 0.0)
            couple_out[height, 64 * at : 64 * at + 64, :] = split(matrix)
    for height in range(5):
        down_out[height] = split(down_ref[0, height])


def prepare(dev, couple_top, down_top):
    outs = [shape((6, 256, 128), bf16), shape((5, 64, 128), bf16)]
    return call(
        prepare_body,
        outs,
        scalars() + held(couple_top, down_top),
        held(*outs),
        name="prepare",
    )(dev, couple_top, down_top)


def sides(dev_ref):
    odd = bit_of(dev_ref, 0)
    return 1 - odd, odd


def near_body(first, count, edges, devices, dev_ref, rhs_ref, points_ref, *rest):
    out_ref, kernels, rim_rhs, rim_source, rim_target = rest[-5:]
    leaves = rhs_ref.shape[0]

    def kernel_of(source, target):
        return lax.rsqrt(dot_columns(source, target)).astype(bf16)

    known = {}

    def rows(s):
        if s not in known:
            if s // 8 not in known.setdefault("groups", {}):
                known["groups"][s // 8] = Coordinates(points_ref, s // 8)
            known[s] = known["groups"][s // 8].rows(s % 8)
        return known[s]

    def build(s):
        source, target = rows(s)
        if s + 1 < leaves:
            targets = jnp.concatenate([target, rows(s + 1)[1]], axis=1)
            kernels[s % 2] = kernel_of(source, targets)
        else:
            kernels[s % 2, :, :256] = kernel_of(source, target)

    if edges:
        inner_ref, outer_ref = rest[:2]
        inner_at, outer_at = sides(dev_ref)
        rim_rhs[...] = jnp.zeros(rim_rhs.shape, bf16)
        rim_source[...] = rows(0)[0]
        rim_target[...] = rows(leaves - 1)[1]
        for halo, side in ((inner_ref, inner_at), (outer_ref, outer_at)):

            @pl.when((side == 0) & (dev_ref[0] > 0))
            def _():
                rim_rhs[0, :, :128] = halo[RHS_AT]
                rim_rhs[0, :, 128:] = halo[RHS_AT + 1]
                rim_source[:, :128] = halo[COORD_AT, 0:16, :]
                rim_source[:, 128:] = halo[COORD_AT, 16:32, :]

            @pl.when((side == 1) & (dev_ref[0] < devices - 1))
            def _():
                rim_rhs[1, :, :128] = halo[RHS_AT]
                rim_rhs[1, :, 128:] = halo[RHS_AT + 1]
                rim_target[:, :128] = halo[COORD_AT, 32:48, :]
                rim_target[:, 128:] = halo[COORD_AT, 48:64, :]

    if count > 0:
        build(first)
    for s in range(first, first + count):
        if s + 1 < first + count:
            build(s + 1)
        kernel = kernels[s % 2]
        own = dot(rhs_ref[s], kernel[:, :256])
        if s + 1 < leaves:
            own += dot_rows(rhs_ref[s + 1], kernel[:, 256:])
            out_ref[s + 1] = dot(rhs_ref[s], kernel[:, 256:])
        out_ref[s] = own if s == 0 else out_ref[s] + own

    if edges:
        before = kernel_of(rim_source[...], rows(0)[1])
        after = kernel_of(rows(leaves - 1)[0], rim_target[...])
        out_ref[0] += dot(rim_rhs[0], before)
        out_ref[leaves - 1] += dot_rows(rim_rhs[1], after)


def near(dev, rhs, points, first, count, halos, total):
    args = [rhs, points] + halos
    out = shape(rhs.shape, f32)
    aliases = {}
    if total is not None:
        aliases = {len(args) + 1: 0}
        args.append(total)
    return call(
        functools.partial(near_body, first, count, len(halos) > 0, lax.axis_size("leaf")),
        out,
        scalars() + held(*args),
        held(out)[0],
        [
            pltpu.VMEM((2, 256, 512), bf16),
            pltpu.VMEM((2, 64, 256), bf16),
            pltpu.VMEM((16, 256), bf16),
            pltpu.VMEM((16, 256), bf16),
        ],
        name="near_%d" % first,
        aliases=aliases,
    )(dev, *args)


def couple_body(
    dev_ref, list_ref, count_ref, node_list_ref, node_count_ref, leaf_ref, node_ref, inner_ref,
    outer_ref, blocks_ref, node_blocks_ref, gain_ref, node_gain_ref, leaf_hold, node_hold,
):
    leaves = leaf_ref.shape[0]
    groups = node_ref.shape[0]
    low = low_lanes((64, 128))

    def keep(hold, at, doubled):
        doubled = doubled.astype(f32)
        hold[0, at] = jnp.where(low, doubled, 0.0).astype(bf16)
        hold[1, at] = jnp.where(low, 0.0, doubled).astype(bf16)

    for leaf in range(leaves):
        keep(leaf_hold, W0 + leaf, leaf_ref[leaf])
    for node in range(groups):
        keep(node_hold, W1 + node, node_ref[node])
    nothing = jnp.zeros((64, 128), f32)
    keep(leaf_hold, leaves + 2 * W0, nothing)
    keep(node_hold, groups + 2 * W1, nothing)
    inner_side, outer_side = sides(dev_ref)
    for halo, side in ((inner_ref, inner_side), (outer_ref, outer_side)):

        def unpack(hold, at, tile):
            pair = halo[tile].astype(f32)
            turned = pltpu.roll(pair, 64, 1)
            keep(hold, at, jnp.where(low, pair, turned))
            keep(hold, at + 1, jnp.where(low, turned, pair))

        for j in range(4):
            unpack(leaf_hold, side * (leaves + W0) + 2 * j, LEAF_AT + j)
        for j in range(2):
            unpack(node_hold, side * (groups + W1) + 2 * j, NODE_AT + j)

    def picked(hold, lists, counts, row, first, slots, nothing):
        count = counts[row]
        at = [jnp.where(k < count, lists[k, row] - first, nothing) for k in range(slots)]
        return jnp.concatenate(
            [hold[0, at[2 * j]] + hold[1, at[2 * j + 1]] for j in range(slots // 2)], axis=1
        )

    def group(g, _):
        for b in range(8):
            row = g * 8 + b
            values = picked(
                leaf_hold, list_ref, count_ref, row, dev_ref[0] * leaves - W0, 8, leaves + 2 * W0
            )
            gain_ref[row] = dot(values, blocks_ref[row].reshape(512, 64))
        values = picked(
            node_hold, node_list_ref, node_count_ref, g, dev_ref[0] * groups - W1, 4, groups + 2 * W1
        )
        node_gain_ref[g] = dot(values, node_blocks_ref[g].reshape(256, 64))
        return 0

    for g in range(groups):
        group(g, 0)


def couple(dev, lists, counts, node_lists, node_counts, leaf, node, inner, outer, blocks, node_blocks):
    leaves, groups = leaf.shape[0], node.shape[0]
    outs = [shape((leaves, 64, 64), f32), shape((groups, 64, 64), f32)]
    ins = [leaf, node, inner, outer, blocks, node_blocks]
    return call(
        couple_body,
        outs,
        scalars(5) + held(*ins),
        held(*outs),
        [
            pltpu.VMEM((2, leaves + 2 * W0 + 1, 64, 128), bf16),
            pltpu.VMEM((2, groups + 2 * W1 + 1, 64, 128), bf16),
        ],
        name="couple",
    )(dev, lists, counts, node_lists, node_counts, *ins)


def downward_body(
    devices, dev_ref, side_ref, got_1, got_2, got_3, got_4, near_ref, far_ref, across_ref, couple_ref,
    down_ref, down_node_ref, node_gain_ref, gain_ref, transfer_ref, bases_ref, sum_ref, out_ref, bank,
    out, sems,
):
    d = dev_ref[0]
    pick = jnp.where
    bank[0] = jnp.zeros((64, 128), bf16)
    upper = bit_of(dev_ref, 3)
    for height in range(3):
        bank[4 - 3 * upper + height] = got_3[2 + height]
        bank[1 + 3 * upper + height] = side_ref[height]
    bank[7] = got_1[PAIR]
    bank[8] = got_2[FIRST]
    bank[9] = got_2[LAST]
    bank[10] = got_2[PARENT_PAIR]
    bank[11] = got_4[PAIR]
    bank[12] = near_ref[0]
    bank[13] = near_ref[1]
    bank[14] = far_ref[0]
    bank[15] = far_ref[1]
    group = d >> 5
    odd = group & 1
    bank[16 + odd] = across_ref[0]
    bank[17 - odd] = far_ref[2]
    bank[16] = join(bank[16], bank[17])
    before = [pick(d >= 8, 1 + height, 0) for height in range(3)]
    after = [pick(d < devices - 8, 4 + height, 0) for height in range(3)]
    parent = d >> 1
    even = (parent & 1) == 0
    left = [pick(even, pick((parent & 3) == 2, 9, before[0]), 7)]
    right = [pick(even, 7, pick((parent & 3) == 1, 8, after[0]))]
    even = ((d >> 2) & 1) == 0
    left += [pick(even, before[1], 10), before[2]]
    right += [pick(even, 10, after[1]), after[2]]
    even = ((d >> 4) & 1) == 0
    beside_left = [pick(odd == 1, 12 + j, pick(group == 2, 14 + j, 0)) for j in range(2)]
    beside_right = [pick(odd == 0, 12 + j, pick(group == 1, 14 + j, 0)) for j in range(2)]
    left += [pick(even, beside_left[0], 11), beside_left[1], pick(group >= 2, 16, 0)]
    right += [pick(even, 11, beside_right[0]), beside_right[1], pick(group >= 2, 0, 16)]
    gains = []
    for height in range(6):
        tiles = jnp.concatenate([bank[left[height]], bank[right[height]]], axis=1)
        gains.append(fused_halves(dot(tiles, couple_ref[height])))
    value = gains[5]
    for height in range(4, -1, -1):
        value = gains[height] + wide_dot(value, down_ref[height])
    rounded = value.astype(bf16)
    groups = down_node_ref.shape[0]

    def move(g):
        at = pl.ds(g * 8, 8)
        return pltpu.make_async_copy(out.at[at], out_ref.at[at], sems.at[g])

    node_values = [(node_gain_ref[g] + dot(rounded, down_node_ref[g])).astype(bf16) for g in range(groups)]

    def move(g):
        at = pl.ds(g * 8, 8)
        return pltpu.make_async_copy(out.at[at], out_ref.at[at], sems.at[g])

    node_values = [(node_gain_ref[g] + dot(rounded, down_node_ref[g])).astype(bf16) for g in range(groups)]
    for g in range(groups):
        bank[g, :, :64] = node_values[g]

    values = {}

    def early(g):
        values[g] = [
            (gain_ref[g * 8 + b] + dot(node_values[g], transfer_ref[g * 8 + b])).astype(bf16) for b in range(8)
        ]

    early(0)
    for g in range(groups):
        if g + 1 < groups:
            early(g + 1)
        for b in range(8):
            leaf = g * 8 + b
            out[leaf] = (sum_ref[leaf] + dot(values[g][b], bases_ref[leaf])).astype(bf16)
        move(g).start()
    for g in range(groups):
        move(g).wait()


def downward(dev, received, couple_parts, down_parts, down_node, node_gain, gain, transfer, bases, near_sum):
    ins = list(received) + [couple_parts, down_parts, down_node, node_gain, gain, transfer, bases, near_sum]
    out = shape(bases.shape, bf16)
    return call(
        functools.partial(downward_body, lax.axis_size("leaf")),
        out,
        scalars() + held(*ins),
        stored(out)[0],
        [
            pltpu.VMEM((18, 64, 128), bf16),
            pltpu.VMEM(out.shape, bf16),
            pltpu.SemaphoreType.DMA((down_node.shape[0],)),
        ],
        name="downward",
    )(dev, *ins)


def tied(*values):
    return lax.optimization_barrier(values)


def shards(
    rhs, points, upward_leaf_bases, downward_leaf_bases, up_leaf, leaf_down_transfer, couple_leaf,
    list_leaf, count_leaf, up_node, down_node, couple_node, list_node, count_node, up_top, down_top,
    couple_top,
):
    device = lax.axis_index("leaf")
    devices = lax.axis_size("leaf")
    dev = device.astype(jnp.int32).reshape(1)

    def beside(block, size):
        route = [(i, (i + size if i // size % 2 == 1 else i - size) % devices) for i in range(devices)]
        return lax.ppermute(block, "leaf", route)

    def exchange(block, mask):
        return lax.ppermute(block, "leaf", [(i, i ^ mask) for i in range(devices)])

    points = jnp.transpose(points, (1, 0, 2))
    leaf, node, inner_out, outer_out = upward(
        dev, rhs, points, upward_leaf_bases, up_leaf, up_node, up_top
    )
    got = inner = exchange(inner_out, 1)
    if OUTER_AFTER < 0:
        outer = beside(outer_out, 1)
    near_sum = near(dev, rhs, points, 0, PARTS[0], [], None)
    done = PARTS[0]
    own = inner_out
    received = []
    for k in range(4):
        got, near_sum = tied(got, near_sum)
        own, *edges = level_call(k, dev, own, got, up_top)
        got = exchange(own, PARTNERS[k])
        received.append(got)
        if k == 2:
            side_out = edges[0]
        if k == SIDE_AFTER:
            side_out, own = tied(side_out, own)
            side = beside(side_out, 8)
        if k == OUTER_AFTER:
            outer_out, own = tied(outer_out, own)
            outer = beside(outer_out, 1)
        near_sum, own = tied(near_sum, own)
        if PARTS[k + 1] > 0:
            near_sum = near(dev, rhs, points, done, PARTS[k + 1], [], near_sum)
            done += PARTS[k + 1]
        if k == COUPLE_AFTER:
            leaf, outer, own = tied(leaf, outer, own)
            gain, node_gain = couple(
                dev, list_leaf.T, count_leaf, list_node.T, count_node, leaf, node, inner, outer,
                couple_leaf, couple_node,
            )
            near_sum, gain = tied(near_sum, gain)
        if k == 2:
            couple_top, _ = tied(couple_top, own)
            couple_parts, down_parts = prepare(dev, couple_top, down_top)
            near_sum, couple_parts = tied(near_sum, couple_parts)
    got, near_sum, outer, side = tied(got, near_sum, outer, side)
    near_out, far_out, across_out = level_call(4, dev, own, got, up_top)
    last = [exchange(near_out, 32), exchange(far_out, 96), exchange(across_out, 64)]
    near_sum, near_out = tied(near_sum, near_out)
    near_sum = near(dev, rhs, points, done, PARTS[5], [inner, outer], near_sum)
    *last, near_sum = tied(*last, near_sum)
    return downward(
        dev, [side] + received + last, couple_parts, down_parts,
        down_node, node_gain, gain, leaf_down_transfer, downward_leaf_bases, near_sum,
    )


OUTER_AFTER = 0
COUPLE_AFTER = 3
SIDE_AFTER = 2
PARTS = (11, 14, 14, 12, 0, 13)


def solution(mesh):
    placed = tuple(P("leaf") for _ in range(17))
    return jax.shard_map(
        shards, mesh=mesh, in_specs=placed, out_specs=P("leaf"), check_vma=False
    )
```
